256 devices in a mesh: group: 8 (over z), dev: 32 (over x, y, core).
Axes of the slice: x: 4, y: 4, z: 8, core: 2. Of those that a mesh axis runs over, the one named last changes fastest.
Arguments:
- embeddings: bfloat16 [229376, 768], P(('group', 'dev')), may hold values from -96 to 96
- assignment: int32 [229376, 1], P(('group', 'dev')), may hold values from 0 to 31; in each aligned block of 896 rows (0 to 895, 896 to 1791, ...) at most 56 rows name the same one
- owner_of: int32 [32], replicated, may hold values from 0 to 31, each once
- pair_on: int32 [2, 256], P(None, ('group', 'dev')), may hold values 0 or 1
Outputs:
- best_match: float32 [229376], P(('group', 'dev'))
The draws below stay inside these ranges and needn't reach their ends.
Inputs may be any that keep to these rules, and one draw needn't show every extreme that they name: `assignment`: each storage shard of 896 rows holds at most 56 rows of any one cluster, and some shard holds exactly 56 rows of some cluster. `owner_of`: each owner index appears exactly once.
All inputs are finite; a program needn't handle non-finite values. No bound on the sum of `pair_on` on one device may be relied on, other than what follows from the above.
Results may differ from the reference program's by a relative error of at most 0.00091.
Values may be sent and summed in bfloat16 or wider, within the bound.
A program may use at most 128 MiB of HBM per device.

```python
import math
import jax
import jax.numpy as jnp
import numpy as np
from jax import lax

D = 768
ROW_DEV = 896
ROUNDS = 2
CAP = 56
SLOTS = 1792
CLUSTERS = 32
ROWS = 229376
N_GROUP = 8
N_DEV = 32
DEVICES = 256


def draw_embeddings(key, part):
    key = jax.random.fold_in(key, 11)
    key_dir, key_str, key_noise = jax.random.split(key, 3)
    direction = jnp.clip(jax.random.normal(key_dir, (D,), jnp.float32), -3.0, 3.0)
    spread = jax.random.uniform(key_str, (ROWS, 1), jnp.float32)
    strength = jnp.exp(-3.0 + 4.0 * spread ** 24)
    noise = jnp.clip(jax.random.normal(key_noise, (ROWS, D), jnp.float32), -4.0, 4.0)
    return (noise + strength * direction[None, :]).astype(jnp.bfloat16)


def place_ends(values, key, low, largest):
    spot = [jax.random.randint(jax.random.fold_in(key, axis), (), 0, length) for axis, length in enumerate(values.shape)]
    widest = values.shape.index(max(values.shape))
    neighbour = spot[:widest] + [(spot[widest] + 1) % values.shape[widest]] + spot[widest + 1:]
    return values.at[tuple(spot)].set(low).at[tuple(neighbour)].set(largest)


def deal_out(own_key, own, number, rows, count, top, bound, skew):
    order = jax.random.permutation(own_key, count)
    packed, common = load_shares(count, rows * top, bound, skew, True), load_shares(count, rows * top, bound, skew, False)
    places = jnp.arange(count)

    def named(lengths, rotation):
        used = int((lengths > 0).sum())
        fixed = max(1, used // 4)
        moved = fixed + (places - fixed + rotation * (used - fixed)) % max(1, count - fixed)
        return jnp.zeros((count,), jnp.int32).at[order[jnp.where(places < fixed, places, moved)]].set(jnp.asarray(lengths, jnp.int32))

    lengths = jnp.where(number % 4 == 0, named(packed, number // 4), named(common, number - number // 4 - 1))
    mixed = jax.random.permutation(jax.random.fold_in(own, 3), count)
    source_of, receiver = mixed[0:count // 2 * 2:2], mixed[1:count // 2 * 2:2]
    margin = jnp.minimum(lengths[source_of] - 1, bound - lengths[receiver]) // 2
    margin = jnp.where((source_of == order[0]) | (receiver == order[0]) | (lengths[receiver] == 0), 0, jnp.maximum(margin, 0))
    moved = jax.random.randint(jax.random.fold_in(own, 4), (count // 2,), 0, 1 << 20) % (margin + 1)
    lengths = lengths.at[source_of].add(-moved).at[receiver].add(moved)
    labels = jnp.searchsorted(jnp.cumsum(lengths), jnp.arange(rows * top), side="right").astype(jnp.int32)
    table = labels.reshape(top, rows).T
    table = table[jax.random.permutation(jax.random.fold_in(own, 1), rows)]
    rotation = jax.random.randint(jax.random.fold_in(own, 2), (rows, 1), 0, top)
    return jnp.take_along_axis(table, (jnp.arange(top)[None, :] + rotation) % top, axis=1)


def load_shares(amount, total, most, slope, full):
    loads = [(1 << 20) // math.isqrt(standing ** slope) + 1 for standing in range(1, amount + 1)]
    largest = most if full else min(most, max(-(-total // amount), total * loads[0] // sum(loads)))
    least = 1 if total - largest >= amount - 1 else 0
    given, spare = [largest] + [least] * (amount - 1), total - largest - least * (amount - 1)
    while spare > 0:
        candidates = [i for i in range(1, amount) if given[i] < largest] or [i for i in range(1, amount) if given[i] < most]
        whole, left = sum([loads[i] for i in candidates]), spare
        for i in candidates:
            addition = min(most - given[i], max(1, left * loads[i] // whole), spare)
            given[i] = given[i] + addition
            spare = spare - addition
    return np.array(given)


def setup_inputs(seed: int = 0) -> dict:
    arg_keys = jax.random.split(jax.random.key(seed), 5)
    embeddings = draw_embeddings(jax.random.fold_in(arg_keys[4], 71), 0)
    assignment_keys = jax.random.split(jax.random.fold_in(arg_keys[1], 1), ROWS // ROW_DEV)
    assignment_turns = jax.random.permutation(jax.random.fold_in(arg_keys[1], 3), ROWS // ROW_DEV)
    assignment = jax.vmap(lambda own, number: deal_out(jax.random.fold_in(arg_keys[1], 2), own, number, ROW_DEV, CLUSTERS, 1, CAP, 2))(assignment_keys, assignment_turns).reshape((ROWS, 1))
    owner_of = jax.random.permutation(arg_keys[2], CLUSTERS).astype(jnp.int32)
    pair_on = place_ends((jax.random.randint(arg_keys[3], (ROUNDS, DEVICES), 0, 4) < 3).astype(jnp.int32), jax.random.fold_in(arg_keys[3], 1), 0, 1)
    return dict(embeddings=embeddings, assignment=assignment, owner_of=owner_of, pair_on=pair_on)


def pair_maxima(left_rows, left_live, right_rows, right_live, skip_self):
    similar = jnp.dot(left_rows, right_rows.T, preferred_element_type=jnp.float32)
    allowed = (left_live[:, None] > 0) & (right_live[None, :] > 0)
    if skip_self:
        allowed = allowed & (jnp.arange(left_rows.shape[0])[:, None] != jnp.arange(right_rows.shape[0])[None, :])
    similar = jnp.where(allowed, similar, -2.0)
    return (lax.optimization_barrier(jnp.max(similar, axis=1)), lax.optimization_barrier(jnp.max(similar, axis=0)))

def reference(embeddings, assignment, owner_of, pair_on):
    values = embeddings.astype(jnp.float32)
    unit_rows = (values * lax.rsqrt(lax.optimization_barrier(jnp.sum(values * values, axis=1, keepdims=True)) + 1e-06)).astype(jnp.bfloat16)
    owners = owner_of[assignment[:, 0]].astype(jnp.int32).reshape(N_GROUP, N_DEV, ROW_DEV)
    one_hot = (owners[..., None] == jnp.arange(N_DEV, dtype=jnp.int32)).astype(jnp.int32)
    slot_ids = lax.optimization_barrier(jnp.sum((jnp.cumsum(one_hot, axis=2) - 1) * one_hot, axis=3)).astype(jnp.int32)
    places = (jnp.arange(N_DEV, dtype=jnp.int32)[None, :, None] * CAP + slot_ids).astype(jnp.int32)
    group_ids = jnp.broadcast_to(jnp.arange(N_GROUP, dtype=jnp.int32)[:, None, None], owners.shape)
    blocks = jnp.zeros((N_GROUP, N_DEV, SLOTS, D), jnp.bfloat16).at[group_ids, owners, places].set(unit_rows.reshape(N_GROUP, N_DEV, ROW_DEV, D))
    presence = jnp.zeros((N_GROUP, N_DEV, SLOTS), jnp.float32).at[group_ids, owners, places].set(1.0)
    switches = pair_on.reshape(ROUNDS, N_GROUP, N_DEV) > 0
    flat_blocks = blocks.reshape(N_GROUP * N_DEV, SLOTS, D)
    flat_live = presence.reshape(N_GROUP * N_DEV, SLOTS)

    def own_term(triple):
        return pair_maxima(triple[0], triple[1], triple[0], triple[1], True)[0]
    leading = lax.map(own_term, (flat_blocks, flat_live)).reshape(N_GROUP, N_DEV, SLOTS)
    leading = jnp.maximum(leading, -1.0)

    def cross_term(triple):
        return pair_maxima(triple[0], triple[1], triple[2], triple[3], False)
    for round_id, shift_by in enumerate((1, N_GROUP // 2)):
        partner = jnp.roll(blocks, shift_by, axis=0).reshape(N_GROUP * N_DEV, SLOTS, D)
        partner_live = jnp.roll(presence, shift_by, axis=0).reshape(N_GROUP * N_DEV, SLOTS)
        row_part, col_part = lax.map(cross_term, (flat_blocks, flat_live, partner, partner_live))
        row_part = row_part.reshape(N_GROUP, N_DEV, SLOTS)
        col_part = col_part.reshape(N_GROUP, N_DEV, SLOTS)
        on_here = switches[round_id][..., None]
        on_there = jnp.roll(switches[round_id], -shift_by, axis=0)[..., None]
        leading = jnp.maximum(leading, jnp.where(on_here, row_part, -2.0))
        leading = jnp.maximum(leading, jnp.where(on_there, jnp.roll(col_part, -shift_by, axis=0), -2.0))
    per_row = leading[group_ids, owners, places]
    return per_row.reshape(ROWS)
```

```python
import functools

import jax
import jax.numpy as jnp
from jax import lax
from jax.experimental import pallas as pl
from jax.experimental.pallas import tpu as pltpu
from jax.sharding import PartitionSpec as P

MESH = pl.DeviceIdType.MESH
SIDE = 4
CHIPS = SIDE * SIDE
OFFSETS = (
    (0, 0), (1, 0), (0, 1), (3, 0), (0, 3), (1, 1), (3, 3), (1, 3),
    (3, 1), (2, 0), (0, 2), (2, 2), (1, 2), (2, 1), (3, 2), (2, 3),
)
MARK = 4.0
DEAD = -8.0
COLS = 256


def kernel(cap, emb_ref, assign_ref, owner_of_ref, pair_ref, out_ref,
           unit, pack, sib_out, sib_in, outbox, members, near, far,
           best, partial, back_out, back_in, flags, flags_in, ret_out, ret_in,
           sib_sem, a2a_ss, a2a_rs, near_ss, near_rs, far_ss, far_rs,
           back_ss, back_rs, flag_ss, flag_rs, ret_ss, ret_rs):
    rows, width = emb_ref.shape
    chunk = 2 * cap
    total = CHIPS * chunk
    group = lax.axis_index("group")
    dev = lax.axis_index("dev")
    groups = lax.axis_size("group")
    core = lax.rem(dev, 2)
    y = lax.rem(dev // 2, SIDE)
    x = dev // (2 * SIDE)

    def chip_dev(off, sign, to_core):
        cx = lax.rem(x + sign * off[0] + SIDE, SIDE)
        cy = lax.rem(y + sign * off[1] + SIDE, SIDE)
        return (cx * SIDE + cy) * 2 + to_core

    def at_group(shift):
        return (lax.rem(group + shift + groups, groups), dev)

    other = 1 - core
    step = 1 - 2 * core
    half_way = groups // 2
    low = (group == 0) | (group == 2) | (group == 5) | (group == 7)
    sends_far = low == (core == 0)
    takes_far = low == (core == 1)

    barrier = pltpu.get_barrier_semaphore()
    for i, off in enumerate(OFFSETS):
        if i:
            pl.semaphore_signal(barrier, inc=1, device_id=(group, chip_dev(off, 1, core)), device_id_type=MESH)
        pl.semaphore_signal(barrier, inc=1, device_id=(group, chip_dev(off, 1, other)), device_id_type=MESH)
    for shift in (1, -1, half_way):
        pl.semaphore_signal(barrier, inc=1, device_id=at_group(shift), device_id_type=MESH)

    values = emb_ref[...].astype(jnp.float32)
    unit[...] = (values * lax.rsqrt(jnp.sum(values * values, axis=1, keepdims=True) + 1e-06)).astype(jnp.bfloat16)

    assign = assign_ref[...]
    ids = lax.broadcasted_iota(jnp.int32, (32, rows), 0)
    owner = jnp.sum(jnp.where(assign == ids, owner_of_ref[...], 0), axis=0, keepdims=True)
    mine = (owner == ids).astype(jnp.float32)
    before = (lax.broadcasted_iota(jnp.int32, (rows, rows), 0)
              < lax.broadcasted_iota(jnp.int32, (rows, rows), 1)).astype(jnp.float32).astype(jnp.bfloat16)
    counted = jnp.dot(mine.astype(jnp.bfloat16), before, preferred_element_type=jnp.float32)
    slot = jnp.sum(counted * mine, axis=0, keepdims=True).astype(jnp.int32)

    def places(to_core):
        place = jnp.full((1, rows), -1, jnp.int32)
        for i, off in enumerate(OFFSETS):
            place = jnp.where(owner == chip_dev(off, 1, to_core), i * cap + slot, place)
        return place

    def packed(place):
        hits = (place == lax.broadcasted_iota(jnp.int32, (CHIPS * cap, rows), 0)).astype(jnp.float32)
        live = jnp.sum(hits, axis=1, keepdims=True)
        got = jnp.dot(hits.astype(jnp.bfloat16), unit[...], preferred_element_type=jnp.float32)
        lane = lax.broadcasted_iota(jnp.int32, (CHIPS * cap, width), 1)
        return jnp.where((lane == 0) & (live < 0.5), MARK, got)

    place_same = places(core)
    place_other = places(other)
    sib_out[...] = packed(place_other).astype(jnp.bfloat16)

    pl.semaphore_wait(barrier, 2 * CHIPS - 1 + 3)

    sib = pltpu.make_async_remote_copy(
        src_ref=sib_out, dst_ref=sib_in, send_sem=sib_sem.at[0], recv_sem=sib_sem.at[1],
        device_id=(group, chip_dev((0, 0), 1, other)), device_id_type=MESH)
    sib.start()
    on = pair_ref[...].astype(jnp.float32)
    flags[...] = jnp.where(lax.broadcasted_iota(jnp.int32, (8, 128), 0) == 0, on[0:1, 0:1], on[1:2, 0:1])
    flag_copies = []
    for n, shift in enumerate((-1, half_way)):
        copy = pltpu.make_async_remote_copy(
            src_ref=flags, dst_ref=flags_in.at[n], send_sem=flag_ss.at[n], recv_sem=flag_rs.at[n],
            device_id=at_group(shift), device_id_type=MESH)
        copy.start()
        flag_copies.append(copy)

    pack[...] = packed(place_same)
    sib.wait()

    def chunk_of(i):
        top = pack[i * cap:(i + 1) * cap, :]
        return top

    from_sib = sib_in[...].astype(jnp.float32)
    sends = []
    for i, off in enumerate(OFFSETS):
        both = jnp.concatenate([chunk_of(i), from_sib[i * cap:(i + 1) * cap, :]], axis=0).astype(jnp.bfloat16)
        if i == 0:
            members[0:chunk, :] = both
            continue
        here = pl.ds(i * chunk, chunk)
        outbox[i * chunk:(i + 1) * chunk, :] = both
        copy = pltpu.make_async_remote_copy(
            src_ref=outbox.at[here], dst_ref=members.at[here], send_sem=a2a_ss.at[i], recv_sem=a2a_rs.at[i],
            device_id=(group, chip_dev(off, 1, core)), device_id_type=MESH)
        copy.start()
        sends.append(copy)

    def near_copy(i):
        here = pl.ds(i * chunk, chunk)
        return pltpu.make_async_remote_copy(
            src_ref=members.at[here], dst_ref=near.at[here], send_sem=near_ss.at[i], recv_sem=near_rs.at[i],
            device_id=at_group(step), device_id_type=MESH)

    def far_copy(i):
        here = pl.ds(i * chunk, chunk)
        return pltpu.make_async_remote_copy(
            src_ref=members.at[here], dst_ref=far.at[here], send_sem=far_ss.at[i], recv_sem=far_rs.at[i],
            device_id=at_group(half_way), device_id_type=MESH)

    for i in range(CHIPS):
        if i:
            sends[i - 1].wait_recv()
        near_copy(i).start()

        @pl.when(sends_far)
        def _(i=i):
            far_copy(i).start()

    tiles = 4
    height = total // tiles
    per_tile = CHIPS // tiles
    first_lane = (lax.broadcasted_iota(jnp.int32, (8, 128), 1) == 0).astype(jnp.float32).astype(jnp.bfloat16)
    marks = lax.dot_general(first_lane, members[:, 0:128], (((1,), (1,)), ((), ())), preferred_element_type=jnp.float32)
    col_bias = jnp.where(marks[0:1, :] > 2.0, DEAD, 0.0)

    def product(block, t, self_block, column_best):
        left_at = pl.ds(pl.multiple_of(t * height, height), height)
        left = block[left_at, :]
        row_bias = jnp.where(block[left_at, 0:128].astype(jnp.float32)[:, 0:1] > 2.0, DEAD, 0.0)
        row_bias = jnp.broadcast_to(row_bias, (height, COLS))
        lane_best = None
        for n in range(total // COLS):
            cols = slice(n * COLS, (n + 1) * COLS)
            sim = lax.dot_general(left, members[cols, :], (((1,), (1,)), ((), ())), preferred_element_type=jnp.float32)
            down = sim + row_bias
            if self_block:
                row_id = t * height + lax.broadcasted_iota(jnp.int32, (height, COLS), 0)
                col_id = n * COLS + lax.broadcasted_iota(jnp.int32, (height, COLS), 1)
                down = jnp.where(row_id == col_id, DEAD, down)
            else:
                across = sim + col_bias[:, cols]
                across = jnp.maximum(across[:, 0:128], across[:, 128:256])
                lane_best = across if lane_best is None else jnp.maximum(lane_best, across)
            down = jnp.max(down.reshape(height // 8, 8, COLS), axis=0)
            column_best[:, cols] = jnp.maximum(column_best[:, cols], down)
        if not self_block:
            partial[left_at, :] = lane_best

    def fold(into):
        for b in range(total // 128):
            lanes = slice(b * 128, (b + 1) * 128)
            into[:, lanes] = jnp.max(partial[lanes, :].T, axis=0, keepdims=True)

    best[...] = jnp.full(best.shape, DEAD, jnp.float32)

    def own_tile(t, carry):
        product(members, t, True, best.at[0])
        return carry

    lax.fori_loop(0, tiles, own_tile, 0)

    for copy in flag_copies:
        copy.wait()
    near_on = jnp.where(core == 0, flags[0:1, 0:1], flags_in[0, 0:1, 0:1])
    far_on = jnp.maximum(flags[1:2, 0:1], flags_in[1, 1:2, 0:1])

    def near_tile(t, carry):
        def wait(i, c):
            near_copy(i).wait_recv()
            return c

        lax.fori_loop(t * per_tile, (t + 1) * per_tile, wait, 0)
        product(near, t, False, best.at[1])
        return carry

    lax.fori_loop(0, tiles, near_tile, 0)
    fold(back_out.at[0])
    back_out[0] = jnp.where(near_on > 0.5, back_out[0], -2.0)
    near_back = pltpu.make_async_remote_copy(
        src_ref=back_out.at[0], dst_ref=back_in.at[0], send_sem=back_ss.at[0], recv_sem=back_rs.at[0],
        device_id=at_group(-step), device_id_type=MESH)
    near_back.start()
    far_back = pltpu.make_async_remote_copy(
        src_ref=back_out.at[1], dst_ref=back_in.at[1], send_sem=back_ss.at[1], recv_sem=back_rs.at[1],
        device_id=at_group(half_way), device_id_type=MESH)

    @pl.when(takes_far)
    def _():
        def far_tile(t, carry):
            def wait(i, c):
                far_copy(i).wait_recv()
                return c

            lax.fori_loop(t * per_tile, (t + 1) * per_tile, wait, 0)
            product(far, t, False, best.at[2])
            return carry

        lax.fori_loop(0, tiles, far_tile, 0)
        fold(back_out.at[1])
        back_out[1] = jnp.where(far_on > 0.5, back_out[1], -2.0)
        far_back.start()
        back_in[1] = jnp.full((1, total), -2.0, jnp.float32)

    near_back.wait_recv()

    @pl.when(sends_far)
    def _():
        far_back.wait_recv()

    leading = jnp.maximum(jnp.max(best[0], axis=0, keepdims=True), -1.0)
    leading = jnp.maximum(leading, jnp.where(near_on > 0.5, jnp.max(best[1], axis=0, keepdims=True), -2.0))
    leading = jnp.maximum(leading, jnp.where(far_on > 0.5, jnp.max(best[2], axis=0, keepdims=True), -2.0))
    leading = jnp.maximum(leading, jnp.maximum(back_in[0], back_in[1]))

    returns = []
    ret_out[...] = jnp.zeros(ret_out.shape, jnp.float32)
    for i, off in enumerate(OFFSETS):
        for q, to_core in enumerate((core, other)):
            j = 2 * i + q
            ret_out[j, 0:1, 0:cap] = leading[:, j * cap:(j + 1) * cap]
            if j == 0:
                ret_in[0] = ret_out[0]
                continue
            copy = pltpu.make_async_remote_copy(
                src_ref=ret_out.at[j], dst_ref=ret_in.at[j], send_sem=ret_ss.at[j], recv_sem=ret_rs.at[j],
                device_id=(group, chip_dev(off, -1, to_core)), device_id_type=MESH)
            copy.start()
            returns.append(copy)

    index = jnp.full((1, rows), -1, jnp.int32)
    for i, off in enumerate(OFFSETS):
        for q, to_core in enumerate((core, other)):
            index = jnp.where(owner == chip_dev(off, 1, to_core), 2 * i + q, index)
    chosen = (index == ids).astype(jnp.float32).astype(jnp.bfloat16)
    for copy in returns:
        copy.wait_recv()
    got = ret_in[:, 0, :]
    spread = jnp.zeros((128, rows), jnp.float32)
    for _ in range(3):
        part = got.astype(jnp.bfloat16)
        got = got - part.astype(jnp.float32)
        spread = spread + lax.dot_general(part, chosen, (((0,), (0,)), ((), ())), preferred_element_type=jnp.float32)
    pick = lax.broadcasted_iota(jnp.int32, (128, rows), 0) == slot
    out_ref[...] = jnp.sum(jnp.where(pick, spread, 0.0), axis=0, keepdims=True)

    for copy in sends + returns + [near_back]:
        copy.wait_send()
    for i in range(CHIPS):
        near_copy(i).wait_send()

    @pl.when(sends_far)
    def _():
        for i in range(CHIPS):
            far_copy(i).wait_send()

    @pl.when(takes_far)
    def _():
        far_back.wait_send()


def on_device(embeddings, assignment, owner_of, pair_on):
    rows, width = embeddings.shape
    owners = owner_of.shape[0]
    cap = 2 * rows // owners
    total = owners * cap
    half = total // 2
    bf16, f32 = jnp.bfloat16, jnp.float32
    dma = pltpu.SemaphoreType.DMA
    out = pl.pallas_call(
        functools.partial(kernel, cap),
        out_shape=jax.ShapeDtypeStruct((1, rows), f32),
        in_specs=[pl.BlockSpec(memory_space=pltpu.VMEM)] * 4,
        out_specs=pl.BlockSpec(memory_space=pltpu.VMEM),
        scratch_shapes=[
            pltpu.VMEM((rows, width), bf16),
            pltpu.VMEM((half, width), f32),
            pltpu.VMEM((half, width), bf16),
            pltpu.VMEM((half, width), bf16),
            pltpu.VMEM((total, width), bf16),
            pltpu.VMEM((total, width), bf16),
            pltpu.VMEM((total, width), bf16),
            pltpu.VMEM((total, width), bf16),
            pltpu.VMEM((3, 8, total), f32),
            pltpu.VMEM((total, 128), f32),
            pltpu.VMEM((2, 1, total), f32),
            pltpu.VMEM((2, 1, total), f32),
            pltpu.VMEM((8, 128), f32),
            pltpu.VMEM((2, 8, 128), f32),
            pltpu.VMEM((owners, 1, 128), f32),
            pltpu.VMEM((owners, 1, 128), f32),
            dma((2,)),
            dma((CHIPS,)), dma((CHIPS,)),
            dma((CHIPS,)), dma((CHIPS,)),
            dma((CHIPS,)), dma((CHIPS,)),
            dma((2,)), dma((2,)),
            dma((2,)), dma((2,)),
            dma((owners,)), dma((owners,)),
        ],
        compiler_params=pltpu.CompilerParams(
            collective_id=0, has_side_effects=True, vmem_limit_bytes=56 * 2**20),
        cost_estimate=pl.CostEstimate(flops=6 * total * total * width, bytes_accessed=2 * rows * width, transcendentals=0),
        name="semdedup",
    )(embeddings, assignment.reshape(1, rows), owner_of.reshape(owners, 1), pair_on)
    return out.reshape(rows)


def solution(mesh):
    placed = (P(("group", "dev"), None), P(("group", "dev"), None), P(), P(None, ("group", "dev")))
    return jax.shard_map(
        on_device, mesh=mesh, in_specs=placed, out_specs=P(("group", "dev")), check_vma=False
    )
```

```python
import functools

import jax
import jax.numpy as jnp
from jax import lax
from jax.experimental import pallas as pl
from jax.experimental.pallas import tpu as pltpu
from jax.sharding import PartitionSpec as P

MESH = pl.DeviceIdType.MESH
SIDE = 4
CHIPS = SIDE * SIDE
OFFSETS = (
    (0, 0), (1, 0), (0, 1), (3, 0), (0, 3), (1, 1), (3, 3), (1, 3),
    (3, 1), (2, 0), (0, 2), (2, 2), (1, 2), (2, 1), (3, 2), (2, 3),
)
MARK = 4.0
DEAD = -8.0
COLS = 256
PIECES = 4
AT_ONCE = (15, 7)


def kernel(cap, emb_ref, assign_ref, owner_of_ref, pair_ref, out_ref,
           unit, pack, hits_other, hits_same, sib_out, sib_in, outbox, members, near, far,
           code, relayed, unit_in, code_in,
           best, partial, back_out, back_in, flags, flags_in, ret_out, ret_in,
           sib_ss, sib_rs, a2a_ss, a2a_rs, near_ss, near_rs, raw_ss, raw_rs, hop_ss, hop_rs, code_sem,
           back_sem, flag_ss, flag_rs, ret_ss, ret_rs):
    rows, width = emb_ref.shape
    chunk = 2 * cap
    total = CHIPS * chunk
    group = lax.axis_index("group")
    dev = lax.axis_index("dev")
    groups = lax.axis_size("group")
    core = lax.rem(dev, 2)
    y = lax.rem(dev // 2, SIDE)
    x = dev // (2 * SIDE)

    def chip_dev(off, sign, to_core):
        cx = lax.rem(x + sign * off[0] + SIDE, SIDE)
        cy = lax.rem(y + sign * off[1] + SIDE, SIDE)
        return (cx * SIDE + cy) * 2 + to_core

    def at_group(shift):
        return (lax.rem(group + shift + groups, groups), dev)

    other = 1 - core
    step = 1 - 2 * core
    half_way = groups // 2

    def any_of(*numbers):
        hit = group == numbers[0]
        for number in numbers[1:]:
            hit = hit | (group == number)
        return hit

    sends_far = any_of(0, 2, 5, 7)
    takes_far = any_of(1, 3, 4, 6)
    relays = (any_of(0, 2, 3, 5), any_of(2, 4, 5, 7))

    barrier = pltpu.get_barrier_semaphore()
    for i, off in enumerate(OFFSETS):
        if i:
            pl.semaphore_signal(barrier, inc=1, device_id=(group, chip_dev(off, 1, core)), device_id_type=MESH)
        pl.semaphore_signal(barrier, inc=1, device_id=(group, chip_dev(off, 1, other)), device_id_type=MESH)
    far_group = lax.rem(group + half_way, groups)
    for i, off in enumerate(OFFSETS):
        for to_core in (core, other):
            pl.semaphore_signal(barrier, inc=1, device_id=(far_group, chip_dev(off, 1, to_core)), device_id_type=MESH)
    shifts = (1, -1, 3, -3)
    for shift in shifts:
        pl.semaphore_signal(barrier, inc=1, device_id=at_group(shift), device_id_type=MESH)

    values = emb_ref[...].astype(jnp.float32)
    unit[...] = (values * lax.rsqrt(jnp.sum(values * values, axis=1, keepdims=True) + 1e-06)).astype(jnp.bfloat16)

    assign = assign_ref[...]
    ids = lax.broadcasted_iota(jnp.int32, (32, rows), 0)
    owner = jnp.zeros((1, rows), jnp.int32)
    for n in range(owner_of_ref.shape[0]):
        owner = jnp.where(assign == n, owner_of_ref[n], owner)
    mine = (owner == ids).astype(jnp.float32)
    before = (lax.broadcasted_iota(jnp.int32, (rows, rows), 0)
              < lax.broadcasted_iota(jnp.int32, (rows, rows), 1)).astype(jnp.float32).astype(jnp.bfloat16)
    counted = jnp.dot(mine.astype(jnp.bfloat16), before, preferred_element_type=jnp.float32)
    slot = jnp.sum(counted * mine, axis=0, keepdims=True).astype(jnp.int32)

    code[...] = (owner * 64 + slot).astype(jnp.float32)

    piece = rows // (2 * PIECES)

    def raw_copy(way, k):
        return pltpu.make_async_remote_copy(
            src_ref=unit.at[pl.ds((way * PIECES + k) * piece, piece)], dst_ref=relayed.at[way, k],
            send_sem=raw_ss.at[way, k], recv_sem=raw_rs.at[way, k],
            device_id=at_group(-3 if way else 3), device_id_type=MESH)

    def hop_copy(way, k):
        return pltpu.make_async_remote_copy(
            src_ref=relayed.at[way, k], dst_ref=unit_in.at[pl.ds((way * PIECES + k) * piece, piece)],
            send_sem=hop_ss.at[way, k], recv_sem=hop_rs.at[way, k],
            device_id=at_group(-1 if way else 1), device_id_type=MESH)

    code_copy = pltpu.make_async_remote_copy(
        src_ref=code, dst_ref=code_in, send_sem=code_sem.at[0], recv_sem=code_sem.at[1],
        device_id=at_group(half_way), device_id_type=MESH)

    def places(owner, slot, to_core):
        place = jnp.full((1, rows), -1, jnp.int32)
        for i, off in enumerate(OFFSETS):
            place = jnp.where(owner == chip_dev(off, 1, to_core), i * cap + slot, place)
        return place

    def set_hits(into, owner, slot, to_core):
        place = places(owner, slot, to_core)
        into[...] = (place == lax.broadcasted_iota(jnp.int32, (CHIPS * cap, rows), 0)).astype(jnp.float32).astype(jnp.bfloat16)

    def packed(hits, source):
        live = jnp.sum(hits[...].astype(jnp.float32), axis=1, keepdims=True)
        got = jnp.dot(hits[...], source[...], preferred_element_type=jnp.float32)
        lane = lax.broadcasted_iota(jnp.int32, (CHIPS * cap, width), 1)
        return jnp.where((lane == 0) & (live < 0.5), MARK, got)

    def sib_copy(turn):
        return pltpu.make_async_remote_copy(
            src_ref=sib_out.at[turn], dst_ref=sib_in.at[turn], send_sem=sib_ss.at[turn], recv_sem=sib_rs.at[turn],
            device_id=(group, chip_dev((0, 0), 1, other)), device_id_type=MESH)

    def chunk_copy(turn, i):
        here = pl.ds(i * chunk, chunk)
        return pltpu.make_async_remote_copy(
            src_ref=outbox.at[turn, here], dst_ref=(members, far)[turn].at[here],
            send_sem=a2a_ss.at[turn, i], recv_sem=a2a_rs.at[turn, i],
            device_id=(group, chip_dev(OFFSETS[i], 1, core)), device_id_type=MESH)

    def pack_all(turn, source):
        sib_out[turn] = packed(hits_other, source).astype(jnp.bfloat16)
        sib_copy(turn).start()
        pack[...] = packed(hits_same, source)
        sib_copy(turn).wait()
        from_sib = sib_in[turn].astype(jnp.float32)
        for i in range(CHIPS):
            both = jnp.concatenate(
                [pack[i * cap:(i + 1) * cap, :], from_sib[i * cap:(i + 1) * cap, :]], axis=0).astype(jnp.bfloat16)
            if i == 0:
                (members, far)[turn][0:chunk, :] = both
                continue
            outbox[turn, i * chunk:(i + 1) * chunk, :] = both
            if i <= AT_ONCE[turn]:
                chunk_copy(turn, i).start()

    def send_rest(turn):
        for i in range(AT_ONCE[turn] + 1, CHIPS):
            chunk_copy(turn, i).start()

    set_hits(hits_other, owner, slot, other)
    pl.semaphore_wait(barrier, 4 * CHIPS - 1 + len(shifts))

    @pl.when(sends_far)
    def _():
        for k in range(PIECES):
            for way in range(2):
                raw_copy(way, k).start()
        code_copy.start()

    set_hits(hits_same, owner, slot, core)
    pack_all(0, unit)
    flags[...] = jnp.where(lax.broadcasted_iota(jnp.int32, (8, 128), 0) == 0, pair_ref[0, 0], pair_ref[0, 1]).astype(jnp.float32)
    flag_copies = []
    for n, shift in enumerate((-1, half_way)):
        copy = pltpu.make_async_remote_copy(
            src_ref=flags, dst_ref=flags_in.at[n], send_sem=flag_ss.at[n], recv_sem=flag_rs.at[n],
            device_id=at_group(shift), device_id_type=MESH)
        copy.start()
        flag_copies.append(copy)

    @pl.when(takes_far)
    def _():
        code_copy.wait_recv()
        whole = code_in[...].astype(jnp.int32)
        set_hits(hits_other, whole // 64, whole % 64, other)
        set_hits(hits_same, whole // 64, whole % 64, core)

    for k in range(PIECES):
        for way in range(2):
            @pl.when(relays[way])
            def _(way=way, k=k):
                raw_copy(way, k).wait_recv()
                hop_copy(way, k).start()

    def near_copy(i):
        here = pl.ds(i * chunk, chunk)
        return pltpu.make_async_remote_copy(
            src_ref=members.at[here], dst_ref=near.at[here], send_sem=near_ss.at[i], recv_sem=near_rs.at[i],
            device_id=at_group(step), device_id_type=MESH)

    for i in range(1, CHIPS):
        chunk_copy(0, i).wait_recv()
    for i in range(CHIPS):
        near_copy(i).start()

    @pl.when(takes_far)
    def _():
        for k in range(PIECES):
            for way in range(2):
                hop_copy(way, k).wait_recv()
        pack_all(1, unit_in)

    tiles = 4
    height = total // tiles
    per_tile = CHIPS // tiles
    first_lane = (lax.broadcasted_iota(jnp.int32, (8, 128), 1) == 0).astype(jnp.float32).astype(jnp.bfloat16)
    marks = lax.dot_general(first_lane, members[:, 0:128], (((1,), (1,)), ((), ())), preferred_element_type=jnp.float32)
    col_bias = jnp.where(marks[0:1, :] > 2.0, DEAD, 0.0)

    def product(block, t, self_block, column_best):
        left_at = pl.ds(t * height if isinstance(t, int) else pl.multiple_of(t * height, height), height)
        left = block[left_at, :]
        row_bias = jnp.where(block[left_at, 0:128].astype(jnp.float32)[:, 0:1] > 2.0, DEAD, 0.0)
        row_bias = jnp.broadcast_to(row_bias, (height, COLS))
        lane_best = None
        for n in range(total // COLS):
            cols = slice(n * COLS, (n + 1) * COLS)
            sim = lax.dot_general(left, members[cols, :], (((1,), (1,)), ((), ())), preferred_element_type=jnp.float32)
            down = sim + row_bias
            if self_block:
                row_id = t * height + lax.broadcasted_iota(jnp.int32, (height, COLS), 0)
                col_id = n * COLS + lax.broadcasted_iota(jnp.int32, (height, COLS), 1)
                down = jnp.where(row_id == col_id, DEAD, down)
            else:
                across = sim + col_bias[:, cols]
                across = jnp.maximum(across[:, 0:128], across[:, 128:256])
                lane_best = across if lane_best is None else jnp.maximum(lane_best, across)
            down = jnp.max(down.reshape(height // 8, 8, COLS), axis=0)
            column_best[:, cols] = jnp.maximum(column_best[:, cols], down)
        if not self_block:
            partial[left_at, :] = lane_best

    def fold(into):
        for b in range(total // 128):
            lanes = slice(b * 128, (b + 1) * 128)
            into[:, lanes] = jnp.max(partial[lanes, :].T, axis=0, keepdims=True)

    best[...] = jnp.full(best.shape, DEAD, jnp.float32)

    def own_tile(t, carry):
        product(members, t, True, best.at[0])
        return carry

    lax.fori_loop(0, tiles, own_tile, 0)

    @pl.when(takes_far)
    def _():
        send_rest(1)

    for copy in flag_copies:
        copy.wait()
    near_on = jnp.where(core == 0, flags[0:1, 0:1], flags_in[0, 0:1, 0:1])
    far_on = jnp.maximum(flags[1:2, 0:1], flags_in[1, 1:2, 0:1])

    def near_tile(t, carry):
        def wait(i, c):
            near_copy(i).wait_recv()
            return c

        lax.fori_loop(t * per_tile, (t + 1) * per_tile, wait, 0)
        product(near, t, False, best.at[1])
        return carry

    lax.fori_loop(0, tiles, near_tile, 0)
    fold(back_out.at[0])
    back_out[0] = jnp.where(near_on > 0.5, back_out[0], -2.0)
    near_back = pltpu.make_async_remote_copy(
        src_ref=back_out.at[0], dst_ref=back_in, send_sem=back_sem.at[0], recv_sem=back_sem.at[1],
        device_id=at_group(-step), device_id_type=MESH)
    near_back.start()

    def ret_copy(turn, j):
        off, to_core = OFFSETS[j // 2], (core, other)[j % 2]
        to_group = lax.rem(group + half_way, groups) if turn else group
        return pltpu.make_async_remote_copy(
            src_ref=ret_out.at[turn, j], dst_ref=ret_in.at[turn, j], send_sem=ret_ss.at[turn, j], recv_sem=ret_rs.at[turn, j],
            device_id=(to_group, chip_dev(off, -1, to_core)), device_id_type=MESH)

    ret_out[...] = jnp.zeros(ret_out.shape, jnp.float32)

    @pl.when(takes_far)
    def _():
        for t in range(tiles):
            for i in range(max(1, t * per_tile), (t + 1) * per_tile):
                chunk_copy(1, i).wait_recv()
            product(far, t, False, best.at[2])
        fold(back_out.at[1])
        theirs = jnp.where(far_on > 0.5, back_out[1], -2.0)
        for j in range(2 * CHIPS):
            ret_out[1, j, 0:1, 0:cap] = theirs[:, j * cap:(j + 1) * cap]
            ret_copy(1, j).start()
        ret_in[1] = jnp.full(ret_in.shape[1:], -2.0, jnp.float32)

    near_back.wait_recv()
    leading = jnp.maximum(jnp.max(best[0], axis=0, keepdims=True), -1.0)
    leading = jnp.maximum(leading, jnp.where(near_on > 0.5, jnp.max(best[1], axis=0, keepdims=True), -2.0))
    leading = jnp.maximum(leading, jnp.where(far_on > 0.5, jnp.max(best[2], axis=0, keepdims=True), -2.0))
    leading = jnp.maximum(leading, back_in[...])

    for j in range(2 * CHIPS):
        ret_out[0, j, 0:1, 0:cap] = leading[:, j * cap:(j + 1) * cap]
        if j:
            ret_copy(0, j).start()
    ret_in[0, 0] = ret_out[0, 0]

    index = jnp.full((1, rows), -1, jnp.int32)
    for i, off in enumerate(OFFSETS):
        for q, to_core in enumerate((core, other)):
            index = jnp.where(owner == chip_dev(off, 1, to_core), 2 * i + q, index)
    chosen = (index == ids).astype(jnp.float32).astype(jnp.bfloat16)
    for j in range(1, 2 * CHIPS):
        ret_copy(0, j).wait_recv()

    @pl.when(sends_far)
    def _():
        for j in range(2 * CHIPS):
            ret_copy(1, j).wait_recv()

    got = jnp.maximum(ret_in[0, :, 0, :], ret_in[1, :, 0, :])
    spread = jnp.zeros((128, rows), jnp.float32)
    for _ in range(3):
        part = got.astype(jnp.bfloat16)
        got = got - part.astype(jnp.float32)
        spread = spread + lax.dot_general(part, chosen, (((0,), (0,)), ((), ())), preferred_element_type=jnp.float32)
    pick = lax.broadcasted_iota(jnp.int32, (128, rows), 0) == slot
    out_ref[...] = jnp.sum(jnp.where(pick, spread, 0.0), axis=0, keepdims=True)

    near_back.wait_send()
    for j in range(1, 2 * CHIPS):
        ret_copy(0, j).wait_send()
    for i in range(CHIPS):
        near_copy(i).wait_send()
        if i:
            chunk_copy(0, i).wait_send()

    @pl.when(sends_far)
    def _():
        for k in range(PIECES):
            for way in range(2):
                raw_copy(way, k).wait_send()
        code_copy.wait_send()

    for way in range(2):
        @pl.when(relays[way])
        def _(way=way):
            for k in range(PIECES):
                hop_copy(way, k).wait_send()

    @pl.when(takes_far)
    def _():
        for i in range(1, CHIPS):
            chunk_copy(1, i).wait_send()
        for j in range(2 * CHIPS):
            ret_copy(1, j).wait_send()


def on_device(embeddings, assignment, owner_of, pair_on):
    rows, width = embeddings.shape
    owners = owner_of.shape[0]
    cap = 2 * rows // owners
    total = owners * cap
    half = total // 2
    bf16, f32 = jnp.bfloat16, jnp.float32
    dma = pltpu.SemaphoreType.DMA
    out = pl.pallas_call(
        functools.partial(kernel, cap),
        out_shape=jax.ShapeDtypeStruct((1, rows), f32),
        in_specs=[pl.BlockSpec(memory_space=pltpu.VMEM)] * 2 + [pl.BlockSpec(memory_space=pltpu.SMEM)] * 2,
        out_specs=pl.BlockSpec(memory_space=pltpu.VMEM),
        scratch_shapes=[
            pltpu.VMEM((rows, width), bf16),
            pltpu.VMEM((half, width), f32),
            pltpu.VMEM((half, rows), bf16),
            pltpu.VMEM((half, rows), bf16),
            pltpu.VMEM((2, half, width), bf16),
            pltpu.VMEM((2, half, width), bf16),
            pltpu.VMEM((2, total, width), bf16),
            pltpu.VMEM((total, width), bf16),
            pltpu.VMEM((total, width), bf16),
            pltpu.VMEM((total, width), bf16),
            pltpu.VMEM((1, rows), f32),
            pltpu.VMEM((2, PIECES, rows // (2 * PIECES), width), bf16),
            pltpu.VMEM((rows, width), bf16),
            pltpu.VMEM((1, rows), f32),
            pltpu.VMEM((3, 8, total), f32),
            pltpu.VMEM((total, 128), f32),
            pltpu.VMEM((2, 1, total), f32),
            pltpu.VMEM((1, total), f32),
            pltpu.VMEM((8, 128), f32),
            pltpu.VMEM((2, 8, 128), f32),
            pltpu.VMEM((2, owners, 1, 128), f32),
            pltpu.VMEM((2, owners, 1, 128), f32),
            dma((2,)), dma((2,)),
            dma((2, CHIPS)), dma((2, CHIPS)),
            dma((CHIPS,)), dma((CHIPS,)),
            dma((2, PIECES)), dma((2, PIECES)),
            dma((2, PIECES)), dma((2, PIECES)),
            dma((2,)),
            dma((2,)),
            dma((2,)), dma((2,)),
            dma((2, owners)), dma((2, owners)),
        ],
        compiler_params=pltpu.CompilerParams(
            collective_id=0, has_side_effects=True, vmem_limit_bytes=56 * 2**20),
        cost_estimate=pl.CostEstimate(flops=6 * total * total * width, bytes_accessed=2 * rows * width, transcendentals=0),
        name="semdedup",
    )(embeddings, assignment.reshape(1, rows), owner_of, pair_on.reshape(1, 2))
    return out.reshape(rows)


def solution(mesh):
    placed = (P(("group", "dev"), None), P(("group", "dev"), None), P(), P(None, ("group", "dev")))
    return jax.shard_map(
        on_device, mesh=mesh, in_specs=placed, out_specs=P(("group", "dev")), check_vma=False
    )
```

```python
import functools

import jax
import jax.numpy as jnp
from jax import lax
from jax.experimental import pallas as pl
from jax.experimental.pallas import tpu as pltpu
from jax.sharding import PartitionSpec as P

MESH = pl.DeviceIdType.MESH
SIDE = 4
CHIPS = SIDE * SIDE
OFFSETS = (
    (0, 0), (2, 2), (1, 2), (2, 1), (3, 2), (2, 3), (1, 1), (3, 3),
    (1, 3), (3, 1), (2, 0), (0, 2), (1, 0), (0, 1), (3, 0), (0, 3),
)
MARK = 4.0
DEAD = -8.0
COLS = 256
PIECES = 7
AHEAD = 7
NEAR_SENDER = (0, 0, 0, 0, 0, 0, 0)
NEAR_TAKER = (0, 0, 6, 9, 12, 16, 16)
PARTS = (((0, 4), (4, 8), (8, 12), (12, 16)), ((0, 2), (2, 4), (4, 6), (6, 8), (8, 12), (12, 16)))
EARLY = (2, 4, 6)


def kernel(cap, emb_ref, assign_ref, owner_of_ref, pair_ref, out_ref,
           unit, in_order, hits_other, hits_same, sib_out, sib_in, outbox, members, near, far,
           base_out, relayed, unit_in, base_in,
           best, partial, back_out, back_in, flags, flags_in, ret_out, ret_in,
           sib_ss, sib_rs, a2a_ss, a2a_rs, near_ss, near_rs, raw_ss, raw_rs, hop_ss, hop_rs, base_sem,
           back_sem, flag_ss, flag_rs, ret_ss, ret_rs):
    rows, width = emb_ref.shape
    chunk = 2 * cap
    total = CHIPS * chunk
    group = lax.axis_index("group")
    dev = lax.axis_index("dev")
    groups = lax.axis_size("group")
    core = lax.rem(dev, 2)
    y = lax.rem(dev // 2, SIDE)
    x = dev // (2 * SIDE)

    def chip_dev(off, sign, to_core):
        cx = lax.rem(x + sign * off[0] + SIDE, SIDE)
        cy = lax.rem(y + sign * off[1] + SIDE, SIDE)
        return (cx * SIDE + cy) * 2 + to_core

    def at_group(shift):
        return (lax.rem(group + shift + groups, groups), dev)

    other = 1 - core
    step = 1 - 2 * core
    half_way = groups // 2

    def any_of(*numbers):
        hit = group == numbers[0]
        for number in numbers[1:]:
            hit = hit | (group == number)
        return hit

    def by_group(table):
        return sum((group == g).astype(jnp.int32) * value for g, value in table.items())

    ways = ({0: 2, 2: 5, 5: 7, 7: 0}, {0: 7, 7: 5, 5: 2, 2: 0})
    sends_far = any_of(0, 2, 5, 7)
    takes_far = any_of(1, 3, 4, 6)
    first_hop = [by_group(way) for way in ways]
    second_hop = [by_group({way[g]: (g + half_way) % groups for g in way}) for way in ways]
    came_from = [by_group({(g + half_way) % groups: way[g] for g in way}) for way in ways]

    barrier = pltpu.get_barrier_semaphore()
    for i, off in enumerate(OFFSETS):
        if i:
            pl.semaphore_signal(barrier, inc=1, device_id=(group, chip_dev(off, 1, core)), device_id_type=MESH)
        pl.semaphore_signal(barrier, inc=1, device_id=(group, chip_dev(off, 1, other)), device_id_type=MESH)
    far_group = lax.rem(group + half_way, groups)
    for i, off in enumerate(OFFSETS):
        for to_core in (core, other):
            pl.semaphore_signal(barrier, inc=1, device_id=(far_group, chip_dev(off, 1, to_core)), device_id_type=MESH)
    for shift in (1, -1):
        pl.semaphore_signal(barrier, inc=1, device_id=at_group(shift), device_id_type=MESH)

    @pl.when(sends_far)
    def _():
        for way in range(2):
            pl.semaphore_signal(barrier, inc=1, device_id=(first_hop[way], dev), device_id_type=MESH)
            pl.semaphore_signal(barrier, inc=2, device_id=(second_hop[way], dev), device_id_type=MESH)

    @pl.when(takes_far)
    def _():
        for way in range(2):
            pl.semaphore_signal(barrier, inc=1, device_id=(came_from[way], dev), device_id_type=MESH)

    values = emb_ref[...].astype(jnp.float32)
    unit[...] = (values * lax.rsqrt(jnp.sum(values * values, axis=1, keepdims=True) + 1e-06)).astype(jnp.bfloat16)

    assign = assign_ref[...]
    ids = lax.broadcasted_iota(jnp.int32, (32, rows), 0)
    owner = jnp.zeros((1, rows), jnp.int32)
    for n in range(owner_of_ref.shape[0]):
        owner = jnp.where(assign == n, owner_of_ref[n], owner)
    index = jnp.full((1, rows), -1, jnp.int32)
    for i, off in enumerate(OFFSETS):
        for q, to_core in enumerate((core, other)):
            index = jnp.where(owner == chip_dev(off, 1, to_core), 2 * i + q, index)
    chosen = (index == ids).astype(jnp.float32)
    before = (lax.broadcasted_iota(jnp.int32, (128, 128), 0)
              < lax.broadcasted_iota(jnp.int32, (128, 128), 1)).astype(jnp.float32).astype(jnp.bfloat16)
    blocks = [chosen[:, n * 128:(n + 1) * 128] for n in range(rows // 128)]
    counted = jnp.dot(jnp.concatenate(blocks, axis=0).astype(jnp.bfloat16), before, preferred_element_type=jnp.float32)
    earlier = jnp.zeros((32, 1), jnp.float32)
    slots = []
    for n, block in enumerate(blocks):
        inside = counted[n * 32:(n + 1) * 32, :] + earlier
        slots.append(jnp.sum(inside * block, axis=0, keepdims=True))
        earlier = earlier + jnp.sum(block, axis=1, keepdims=True)
    slot = jnp.concatenate(slots, axis=1).astype(jnp.int32)
    above = (lax.broadcasted_iota(jnp.int32, (32, 32), 1)
             < lax.broadcasted_iota(jnp.int32, (32, 32), 0)).astype(jnp.float32).astype(jnp.bfloat16)
    base_out[...] = jnp.dot(
        above, jnp.broadcast_to(earlier, (32, 128)).astype(jnp.bfloat16), preferred_element_type=jnp.float32)

    piece = rows // (2 * PIECES)

    def raw_copy(way, k):
        return pltpu.make_async_remote_copy(
            src_ref=in_order.at[pl.ds((2 * k + way) * piece, piece)], dst_ref=relayed.at[way, k],
            send_sem=raw_ss.at[way, k], recv_sem=raw_rs.at[way, k],
            device_id=(first_hop[way], dev), device_id_type=MESH)

    def hop_copy(way, k):
        return pltpu.make_async_remote_copy(
            src_ref=relayed.at[way, k], dst_ref=unit_in.at[pl.ds((2 * k + way) * piece, piece)],
            send_sem=hop_ss.at[way, k], recv_sem=hop_rs.at[way, k],
            device_id=(second_hop[way], dev), device_id_type=MESH)

    base_copy = pltpu.make_async_remote_copy(
        src_ref=base_out, dst_ref=base_in, send_sem=base_sem.at[0], recv_sem=base_sem.at[1],
        device_id=at_group(half_way), device_id_type=MESH)

    def set_hits(index, slot):
        position = lax.broadcasted_iota(jnp.int32, (CHIPS * cap, rows), 0)
        for q, into in enumerate((hits_same, hits_other)):
            place = jnp.where(index % 2 == q, index // 2 * cap + slot, -1)
            into[...] = (place == position).astype(jnp.float32).astype(jnp.bfloat16)

    def packed(hits, source, part, depth):
        some = hits[part[0] * cap:part[1] * cap, 0:depth]
        live = jnp.sum(some.astype(jnp.float32), axis=1, keepdims=True)
        got = jnp.dot(some, source[0:depth, :], preferred_element_type=jnp.float32)
        lane = lax.broadcasted_iota(jnp.int32, got.shape, 1)
        return jnp.where((lane == 0) & (live < 0.5), MARK, got)

    def sib_copy(turn, n):
        first, last = PARTS[turn][n]
        here = pl.ds(first * cap, (last - first) * cap)
        return pltpu.make_async_remote_copy(
            src_ref=sib_out.at[turn, here], dst_ref=sib_in.at[turn, here],
            send_sem=sib_ss.at[turn, n], recv_sem=sib_rs.at[turn, n],
            device_id=(group, chip_dev((0, 0), 1, other)), device_id_type=MESH)

    def chunk_copy(turn, i):
        here = pl.ds(i * chunk, chunk)
        return pltpu.make_async_remote_copy(
            src_ref=outbox.at[turn, here], dst_ref=(members, far)[turn].at[here],
            send_sem=a2a_ss.at[turn, i], recv_sem=a2a_rs.at[turn, i],
            device_id=(group, chip_dev(OFFSETS[i], 1, core)), device_id_type=MESH)

    def give_sibling(turn, source, n, depth=rows):
        part = PARTS[turn][n]
        sib_out[turn, part[0] * cap:part[1] * cap, :] = packed(hits_other, source, part, depth).astype(jnp.bfloat16)
        sib_copy(turn, n).start()

    def make_part(turn, source, n, depth=rows):
        part = PARTS[turn][n]
        own = packed(hits_same, source, part, depth)
        sib_copy(turn, n).wait()
        from_sib = sib_in[turn, part[0] * cap:part[1] * cap, :].astype(jnp.float32)
        for i in range(*part):
            here = slice((i - part[0]) * cap, (i - part[0] + 1) * cap)
            both = jnp.concatenate([own[here, :], from_sib[here, :]], axis=0).astype(jnp.bfloat16)
            if i == 0:
                (members, far)[turn][0:chunk, :] = both
            else:
                outbox[turn, i * chunk:(i + 1) * chunk, :] = both

    def send_part(turn, n):
        for i in range(*PARTS[turn][n]):
            if i:
                chunk_copy(turn, i).start()

    def send_all(turn, source, first):
        last = len(PARTS[turn])
        for n in range(first, min(first + 2, last)):
            give_sibling(turn, source, n)
        for n in range(first, last):
            make_part(turn, source, n)
            send_part(turn, n)
            if n + 2 < last:
                give_sibling(turn, source, n + 2)

    pl.semaphore_wait(barrier, 4 * CHIPS - 1 + 2 + 4)

    @pl.when(sends_far)
    def _():
        base_copy.start()
        sorted_at = jnp.sum(chosen * base_out[:, 0:1], axis=0, keepdims=True).astype(jnp.int32) + slot
        sent = 0
        for n in range(2):
            here = slice(n * rows // 2, (n + 1) * rows // 2)
            position = lax.broadcasted_iota(jnp.int32, (rows // 2, rows), 0) + n * rows // 2
            order = (sorted_at == position).astype(jnp.float32).astype(jnp.bfloat16)
            in_order[here, :] = jnp.dot(order, unit[...], preferred_element_type=jnp.float32).astype(jnp.bfloat16)
            while sent < AHEAD and (sent + 1) * 2 * piece <= (n + 1) * rows // 2:
                for way in range(2):
                    raw_copy(way, sent).start()
                sent += 1

    set_hits(index, slot)
    send_all(0, unit, 0)
    flags[...] = jnp.where(lax.broadcasted_iota(jnp.int32, (8, 128), 0) == 0, pair_ref[0, 0], pair_ref[0, 1]).astype(jnp.float32)
    flag_copies = []
    for n, shift in enumerate((-1, half_way)):
        copy = pltpu.make_async_remote_copy(
            src_ref=flags, dst_ref=flags_in.at[n], send_sem=flag_ss.at[n], recv_sem=flag_rs.at[n],
            device_id=at_group(shift), device_id_type=MESH)
        copy.start()
        flag_copies.append(copy)

    def near_copy(i):
        here = pl.ds(i * chunk, chunk)
        return pltpu.make_async_remote_copy(
            src_ref=members.at[here], dst_ref=near.at[here], send_sem=near_ss.at[i], recv_sem=near_rs.at[i],
            device_id=at_group(step), device_id_type=MESH)

    @pl.when(takes_far)
    def _():
        base_copy.wait_recv()
        base = base_in[:, 0:1].astype(jnp.int32)
        position = lax.broadcasted_iota(jnp.int32, (32, rows), 1)
        begun = base <= position
        far_index = jnp.sum(jnp.where(begun, 1, 0), axis=0, keepdims=True) - 1
        far_slot = position[0:1, :] - jnp.max(jnp.where(begun, base, 0), axis=0, keepdims=True)
        set_hits(far_index, far_slot)

    def send_near(table, k):
        for i in range(table[k - 1] if k else 0, table[k] if k < PIECES else CHIPS):
            if i:
                chunk_copy(0, i).wait_recv()
            near_copy(i).start()

    for k in range(PIECES):
        @pl.when(sends_far)
        def _(k=k):
            for way in range(2):
                raw_copy(way, k).wait_recv()
                hop_copy(way, k).start()
                if k + AHEAD < PIECES:
                    raw_copy(way, k + AHEAD).start()
            send_near(NEAR_SENDER, k)

        @pl.when(takes_far)
        def _(k=k):
            for way in range(2):
                hop_copy(way, k).wait_recv()
            if k + 1 in EARLY:
                give_sibling(1, unit_in, EARLY.index(k + 1), (k + 1) * 2 * piece)
            if k in EARLY:
                make_part(1, unit_in, EARLY.index(k), k * 2 * piece)
                send_part(1, EARLY.index(k))
            send_near(NEAR_TAKER, k)

    @pl.when(sends_far)
    def _():
        send_near(NEAR_SENDER, PIECES)

    @pl.when(takes_far)
    def _():
        send_near(NEAR_TAKER, PIECES)
        send_all(1, unit_in, len(EARLY))

    tiles = 4
    height = total // tiles
    per_tile = CHIPS // tiles
    first_lane = (lax.broadcasted_iota(jnp.int32, (8, 128), 1) == 0).astype(jnp.float32).astype(jnp.bfloat16)
    marks = lax.dot_general(first_lane, members[:, 0:128], (((1,), (1,)), ((), ())), preferred_element_type=jnp.float32)
    col_bias = jnp.where(marks[0:1, :] > 2.0, DEAD, 0.0)

    def product(block, t, kept, column_best):
        self_block = kept is None
        left_at = pl.ds(t * height if isinstance(t, int) else pl.multiple_of(t * height, height), height)
        left = block[left_at, :]
        row_bias = jnp.where(block[left_at, 0:128].astype(jnp.float32)[:, 0:1] > 2.0, DEAD, 0.0)
        row_bias = jnp.broadcast_to(row_bias, (height, COLS))
        lane_best = None
        for n in range(total // COLS):
            cols = slice(n * COLS, (n + 1) * COLS)
            sim = lax.dot_general(left, members[cols, :], (((1,), (1,)), ((), ())), preferred_element_type=jnp.float32)
            down = sim + row_bias
            if self_block:
                row_id = t * height + lax.broadcasted_iota(jnp.int32, (height, COLS), 0)
                col_id = n * COLS + lax.broadcasted_iota(jnp.int32, (height, COLS), 1)
                down = jnp.where(row_id == col_id, DEAD, down)
            else:
                across = sim + col_bias[:, cols]
                across = jnp.maximum(across[:, 0:128], across[:, 128:256])
                lane_best = across if lane_best is None else jnp.maximum(lane_best, across)
            down = jnp.max(down.reshape(height // 8, 8, COLS), axis=0)
            column_best[:, cols] = jnp.maximum(column_best[:, cols], down)
        if not self_block:
            kept[left_at, :] = lane_best

    def fold(kept, into, t):
        for b in range(t * height // 128, (t + 1) * height // 128):
            lanes = slice(b * 128, (b + 1) * 128)
            into[:, lanes] = jnp.max(kept[lanes, :].T, axis=0, keepdims=True)

    best[...] = jnp.full(best.shape, DEAD, jnp.float32)

    def own_tile(t, carry):
        product(members, t, None, best.at[0])
        return carry

    lax.fori_loop(0, tiles, own_tile, 0)

    for copy in flag_copies:
        copy.wait()
    near_on = jnp.where(core == 0, flags[0:1, 0:1], flags_in[0, 0:1, 0:1])
    far_on = jnp.maximum(flags[1:2, 0:1], flags_in[1, 1:2, 0:1])

    near_back = pltpu.make_async_remote_copy(
        src_ref=back_out.at[0], dst_ref=back_in, send_sem=back_sem.at[0], recv_sem=back_sem.at[1],
        device_id=at_group(-step), device_id_type=MESH)

    def ret_copy(turn, j):
        off, to_core = OFFSETS[j // 2], (core, other)[j % 2]
        to_group = lax.rem(group + half_way, groups) if turn else group
        return pltpu.make_async_remote_copy(
            src_ref=ret_out.at[turn, j], dst_ref=ret_in.at[turn, j], send_sem=ret_ss.at[turn, j], recv_sem=ret_rs.at[turn, j],
            device_id=(to_group, chip_dev(off, -1, to_core)), device_id_type=MESH)

    ret_out[...] = jnp.zeros(ret_out.shape, jnp.float32)

    for t in range(tiles):
        for i in range(t * per_tile, (t + 1) * per_tile):
            near_copy(i).wait_recv()
        product(near, t, partial.at[0], best.at[1])
        fold(partial.at[0], back_out.at[0], t)
        if t == tiles - 1:
            back_out[0] = jnp.where(near_on > 0.5, back_out[0], -2.0)
            near_back.start()

        @pl.when(takes_far)
        def _(t=t):
            for i in range(max(1, t * per_tile), (t + 1) * per_tile):
                chunk_copy(1, i).wait_recv()
            product(far, t, partial.at[1], best.at[2])
            fold(partial.at[1], back_out.at[1], t)

    @pl.when(takes_far)
    def _():
        theirs = jnp.where(far_on > 0.5, back_out[1], -2.0)
        for j in range(2 * CHIPS):
            ret_out[1, j, 0:1, 0:cap] = theirs[:, j * cap:(j + 1) * cap]
            ret_copy(1, j).start()
        ret_in[1] = jnp.full(ret_in.shape[1:], -2.0, jnp.float32)

    near_back.wait_recv()
    leading = jnp.maximum(jnp.max(best[0], axis=0, keepdims=True), -1.0)
    leading = jnp.maximum(leading, jnp.where(near_on > 0.5, jnp.max(best[1], axis=0, keepdims=True), -2.0))
    leading = jnp.maximum(leading, jnp.where(far_on > 0.5, jnp.max(best[2], axis=0, keepdims=True), -2.0))
    leading = jnp.maximum(leading, back_in[...])

    for j in range(2 * CHIPS):
        ret_out[0, j, 0:1, 0:cap] = leading[:, j * cap:(j + 1) * cap]
        if j:
            ret_copy(0, j).start()
    ret_in[0, 0] = ret_out[0, 0]

    wanted = chosen.astype(jnp.bfloat16)
    for j in range(1, 2 * CHIPS):
        ret_copy(0, j).wait_recv()

    @pl.when(sends_far)
    def _():
        for j in range(2 * CHIPS):
            ret_copy(1, j).wait_recv()

    got = jnp.maximum(ret_in[0, :, 0, :], ret_in[1, :, 0, :])
    spread = jnp.zeros((128, rows), jnp.float32)
    for _ in range(3):
        part = got.astype(jnp.bfloat16)
        got = got - part.astype(jnp.float32)
        spread = spread + lax.dot_general(part, wanted, (((0,), (0,)), ((), ())), preferred_element_type=jnp.float32)
    pick = lax.broadcasted_iota(jnp.int32, (128, rows), 0) == slot
    out_ref[...] = jnp.sum(jnp.where(pick, spread, 0.0), axis=0, keepdims=True)

    near_back.wait_send()
    for j in range(1, 2 * CHIPS):
        ret_copy(0, j).wait_send()
    for i in range(CHIPS):
        near_copy(i).wait_send()
        if i:
            chunk_copy(0, i).wait_send()

    @pl.when(sends_far)
    def _():
        for k in range(PIECES):
            for way in range(2):
                raw_copy(way, k).wait_send()
                hop_copy(way, k).wait_send()
        base_copy.wait_send()

    @pl.when(takes_far)
    def _():
        for i in range(1, CHIPS):
            chunk_copy(1, i).wait_send()
        for j in range(2 * CHIPS):
            ret_copy(1, j).wait_send()


def on_device(embeddings, assignment, owner_of, pair_on):
    rows, width = embeddings.shape
    owners = owner_of.shape[0]
    cap = 2 * rows // owners
    total = owners * cap
    half = total // 2
    bf16, f32 = jnp.bfloat16, jnp.float32
    dma = pltpu.SemaphoreType.DMA
    out = pl.pallas_call(
        functools.partial(kernel, cap),
        out_shape=jax.ShapeDtypeStruct((1, rows), f32),
        in_specs=[pl.BlockSpec(memory_space=pltpu.VMEM)] * 2 + [pl.BlockSpec(memory_space=pltpu.SMEM)] * 2,
        out_specs=pl.BlockSpec(memory_space=pltpu.VMEM),
        scratch_shapes=[
            pltpu.VMEM((rows, width), bf16),
            pltpu.VMEM((rows, width), bf16),
            pltpu.VMEM((half, rows), bf16),
            pltpu.VMEM((half, rows), bf16),
            pltpu.VMEM((2, half, width), bf16),
            pltpu.VMEM((2, half, width), bf16),
            pltpu.VMEM((2, total, width), bf16),
            pltpu.VMEM((total, width), bf16),
            pltpu.VMEM((total, width), bf16),
            pltpu.VMEM((total, width), bf16),
            pltpu.VMEM((owners, 128), f32),
            pltpu.VMEM((2, PIECES, rows // (2 * PIECES), width), bf16),
            pltpu.VMEM((rows, width), bf16),
            pltpu.VMEM((owners, 128), f32),
            pltpu.VMEM((3, 8, total), f32),
            pltpu.VMEM((2, total, 128), f32),
            pltpu.VMEM((2, 1, total), f32),
            pltpu.VMEM((1, total), f32),
            pltpu.VMEM((8, 128), f32),
            pltpu.VMEM((2, 8, 128), f32),
            pltpu.VMEM((2, owners, 1, 128), f32),
            pltpu.VMEM((2, owners, 1, 128), f32),
            dma((2, 6)), dma((2, 6)),
            dma((2, CHIPS)), dma((2, CHIPS)),
            dma((CHIPS,)), dma((CHIPS,)),
            dma((2, PIECES)), dma((2, PIECES)),
            dma((2, PIECES)), dma((2, PIECES)),
            dma((2,)),
            dma((2,)),
            dma((2,)), dma((2,)),
            dma((2, owners)), dma((2, owners)),
        ],
        compiler_params=pltpu.CompilerParams(
            collective_id=0, has_side_effects=True, vmem_limit_bytes=56 * 2**20),
        cost_estimate=pl.CostEstimate(flops=6 * total * total * width, bytes_accessed=2 * rows * width, transcendentals=0),
        name="semdedup",
    )(embeddings, assignment.reshape(1, rows), owner_of, pair_on.reshape(1, 2))
    return out.reshape(rows)


def solution(mesh):
    placed = (P(("group", "dev"), None), P(("group", "dev"), None), P(), P(None, ("group", "dev")))
    return jax.shard_map(
        on_device, mesh=mesh, in_specs=placed, out_specs=P(("group", "dev")), check_vma=False
    )
```

```python
import functools

import jax
import jax.numpy as jnp
from jax import lax
from jax.experimental import pallas as pl
from jax.experimental.pallas import tpu as pltpu
from jax.sharding import PartitionSpec as P

MESH = pl.DeviceIdType.MESH
SIDE = 4
CHIPS = SIDE * SIDE
OFFSETS = (
    (0, 0), (2, 2), (1, 2), (2, 1), (3, 2), (2, 3), (1, 1), (3, 3),
    (1, 3), (3, 1), (2, 0), (0, 2), (1, 0), (0, 1), (3, 0), (0, 3),
)
MARK = 4.0
DEAD = -8.0
COLS = 256
PIECES = 7
AHEAD = 7
NEAR_SENDER = (0, 0, 0, 0, 0, 0, 0)
NEAR_TAKER = (0, 0, 0, 0, 6, 11, 16)
PARTS = (((0, 4), (4, 8), (8, 12), (12, 16)), ((0, 2), (2, 4), (4, 6), (6, 8), (8, 12), (12, 16)))
EARLY = (2, 4, 6)


def kernel(cap, emb_ref, assign_ref, owner_of_ref, pair_ref, out_ref,
           unit, in_order, place, sib_out, sib_in, outbox, members, near, far,
           base_out, relayed, unit_in, base_in,
           best, partial, back_out, back_in, flags, flags_in, ret_out, ret_in,
           sib_ss, sib_rs, a2a_ss, a2a_rs, near_ss, near_rs, raw_ss, raw_rs, hop_ss, hop_rs, base_sem,
           back_sem, flag_ss, flag_rs, ret_ss, ret_rs):
    rows, width = emb_ref.shape
    chunk = 2 * cap
    total = CHIPS * chunk
    group = lax.axis_index("group")
    dev = lax.axis_index("dev")
    groups = lax.axis_size("group")
    core = lax.rem(dev, 2)
    y = lax.rem(dev // 2, SIDE)
    x = dev // (2 * SIDE)

    def chip_dev(off, sign, to_core):
        cx = lax.rem(x + sign * off[0] + SIDE, SIDE)
        cy = lax.rem(y + sign * off[1] + SIDE, SIDE)
        return (cx * SIDE + cy) * 2 + to_core

    def at_group(shift):
        return (lax.rem(group + shift + groups, groups), dev)

    other = 1 - core
    step = 1 - 2 * core
    half_way = groups // 2

    def any_of(*numbers):
        hit = group == numbers[0]
        for number in numbers[1:]:
            hit = hit | (group == number)
        return hit

    def by_group(table):
        return sum((group == g).astype(jnp.int32) * value for g, value in table.items())

    ways = ({0: 2, 2: 5, 5: 7, 7: 0}, {0: 7, 7: 5, 5: 2, 2: 0})
    sends_far = any_of(0, 2, 5, 7)
    takes_far = any_of(1, 3, 4, 6)
    first_hop = [by_group(way) for way in ways]
    second_hop = [by_group({way[g]: (g + half_way) % groups for g in way}) for way in ways]
    came_from = [by_group({(g + half_way) % groups: way[g] for g in way}) for way in ways]

    barrier = pltpu.get_barrier_semaphore()
    for i, off in enumerate(OFFSETS):
        if i:
            pl.semaphore_signal(barrier, inc=1, device_id=(group, chip_dev(off, 1, core)), device_id_type=MESH)
        pl.semaphore_signal(barrier, inc=1, device_id=(group, chip_dev(off, 1, other)), device_id_type=MESH)
    far_group = lax.rem(group + half_way, groups)
    for i, off in enumerate(OFFSETS):
        for to_core in (core, other):
            pl.semaphore_signal(barrier, inc=1, device_id=(far_group, chip_dev(off, 1, to_core)), device_id_type=MESH)
    for shift in (1, -1):
        pl.semaphore_signal(barrier, inc=1, device_id=at_group(shift), device_id_type=MESH)

    @pl.when(sends_far)
    def _():
        for way in range(2):
            pl.semaphore_signal(barrier, inc=1, device_id=(first_hop[way], dev), device_id_type=MESH)
            pl.semaphore_signal(barrier, inc=2, device_id=(second_hop[way], dev), device_id_type=MESH)

    @pl.when(takes_far)
    def _():
        for way in range(2):
            pl.semaphore_signal(barrier, inc=1, device_id=(came_from[way], dev), device_id_type=MESH)

    values = emb_ref[...].astype(jnp.float32)
    unit[...] = (values * lax.rsqrt(jnp.sum(values * values, axis=1, keepdims=True) + 1e-06)).astype(jnp.bfloat16)

    assign = assign_ref[...]
    ids = lax.broadcasted_iota(jnp.int32, (32, rows), 0)
    owner = jnp.zeros((1, rows), jnp.int32)
    for n in range(owner_of_ref.shape[0]):
        owner = jnp.where(assign == n, owner_of_ref[n], owner)
    index = jnp.full((1, rows), -1, jnp.int32)
    for i, off in enumerate(OFFSETS):
        for q, to_core in enumerate((core, other)):
            index = jnp.where(owner == chip_dev(off, 1, to_core), 2 * i + q, index)
    chosen = (index == ids).astype(jnp.float32)
    before = (lax.broadcasted_iota(jnp.int32, (128, 128), 0)
              < lax.broadcasted_iota(jnp.int32, (128, 128), 1)).astype(jnp.float32).astype(jnp.bfloat16)
    blocks = [chosen[:, n * 128:(n + 1) * 128] for n in range(rows // 128)]
    counted = jnp.dot(jnp.concatenate(blocks, axis=0).astype(jnp.bfloat16), before, preferred_element_type=jnp.float32)
    earlier = jnp.zeros((32, 1), jnp.float32)
    slots = []
    for n, block in enumerate(blocks):
        inside = counted[n * 32:(n + 1) * 32, :] + earlier
        slots.append(jnp.sum(inside * block, axis=0, keepdims=True))
        earlier = earlier + jnp.sum(block, axis=1, keepdims=True)
    slot = jnp.concatenate(slots, axis=1).astype(jnp.int32)
    above = (lax.broadcasted_iota(jnp.int32, (32, 32), 1)
             < lax.broadcasted_iota(jnp.int32, (32, 32), 0)).astype(jnp.float32).astype(jnp.bfloat16)
    base_out[...] = jnp.dot(
        above, jnp.broadcast_to(earlier, (32, 128)).astype(jnp.bfloat16), preferred_element_type=jnp.float32)

    piece = rows // (2 * PIECES)

    def raw_copy(way, k):
        return pltpu.make_async_remote_copy(
            src_ref=in_order.at[pl.ds((2 * k + way) * piece, piece)], dst_ref=relayed.at[way, k],
            send_sem=raw_ss.at[way, k], recv_sem=raw_rs.at[way, k],
            device_id=(first_hop[way], dev), device_id_type=MESH)

    def hop_copy(way, k):
        return pltpu.make_async_remote_copy(
            src_ref=relayed.at[way, k], dst_ref=unit_in.at[pl.ds((2 * k + way) * piece, piece)],
            send_sem=hop_ss.at[way, k], recv_sem=hop_rs.at[way, k],
            device_id=(second_hop[way], dev), device_id_type=MESH)

    base_copy = pltpu.make_async_remote_copy(
        src_ref=base_out, dst_ref=base_in, send_sem=base_sem.at[0], recv_sem=base_sem.at[1],
        device_id=at_group(half_way), device_id_type=MESH)

    def set_places(turn, index, slot):
        for q in range(2):
            place[turn, q] = jnp.where(index % 2 == q, index // 2 * cap + slot, -1)

    def packed(turn, q, source, part, depth):
        position = lax.broadcasted_iota(jnp.int32, ((part[1] - part[0]) * cap, depth), 0) + part[0] * cap
        hits = (place[turn, q, :, 0:depth] == position).astype(jnp.float32)
        live = jnp.sum(hits, axis=1, keepdims=True)
        got = jnp.dot(hits.astype(jnp.bfloat16), source[0:depth, :], preferred_element_type=jnp.float32)
        lane = lax.broadcasted_iota(jnp.int32, got.shape, 1)
        return jnp.where((lane == 0) & (live < 0.5), MARK, got)

    def sib_copy(turn, n):
        first, last = PARTS[turn][n]
        here = pl.ds(first * cap, (last - first) * cap)
        return pltpu.make_async_remote_copy(
            src_ref=sib_out.at[turn, here], dst_ref=sib_in.at[turn, here],
            send_sem=sib_ss.at[turn, n], recv_sem=sib_rs.at[turn, n],
            device_id=(group, chip_dev((0, 0), 1, other)), device_id_type=MESH)

    cut = -(-chunk // 32) * 16

    def chunk_copy(turn, i, h):
        here = pl.ds(i * chunk + h * cut, chunk - cut if h else cut)
        return pltpu.make_async_remote_copy(
            src_ref=outbox.at[turn, here], dst_ref=(members, far)[turn].at[here],
            send_sem=a2a_ss.at[turn, i, h], recv_sem=a2a_rs.at[turn, i, h],
            device_id=(group, chip_dev(OFFSETS[i], 1, core)), device_id_type=MESH)

    def chunk_arrived(turn, i):
        for h in range(2):
            chunk_copy(turn, i, h).wait_recv()

    def chunk_left(turn, i):
        for h in range(2):
            chunk_copy(turn, i, h).wait_send()

    def give_sibling(turn, source, n, depth=rows):
        part = PARTS[turn][n]
        sib_out[turn, part[0] * cap:part[1] * cap, :] = packed(turn, 1, source, part, depth).astype(jnp.bfloat16)
        sib_copy(turn, n).start()

    def make_part(turn, source, n, depth=rows):
        part = PARTS[turn][n]
        own = packed(turn, 0, source, part, depth)
        sib_copy(turn, n).wait()
        from_sib = sib_in[turn, part[0] * cap:part[1] * cap, :].astype(jnp.float32)
        for i in range(*part):
            here = slice((i - part[0]) * cap, (i - part[0] + 1) * cap)
            both = jnp.concatenate([own[here, :], from_sib[here, :]], axis=0).astype(jnp.bfloat16)
            if i == 0:
                (members, far)[turn][0:chunk, :] = both
            else:
                outbox[turn, i * chunk:(i + 1) * chunk, :] = both

    def send_half(turn, n, h):
        for i in range(*PARTS[turn][n]):
            if i:
                chunk_copy(turn, i, h).start()

    def send_all(turn, source, first):
        last = len(PARTS[turn])
        for n in range(first, min(first + 2, last)):
            give_sibling(turn, source, n)
        for n in range(first, last):
            make_part(turn, source, n)
            send_half(turn, n, 0)
            if n + 2 < last:
                give_sibling(turn, source, n + 2)
        for n in range(first, last):
            send_half(turn, n, 1)

    pl.semaphore_wait(barrier, 4 * CHIPS - 1 + 2 + 4)

    @pl.when(sends_far)
    def _():
        base_copy.start()
        sorted_at = jnp.sum(chosen * base_out[:, 0:1], axis=0, keepdims=True).astype(jnp.int32) + slot
        sent = 0
        for n in range(2):
            here = slice(n * rows // 2, (n + 1) * rows // 2)
            position = lax.broadcasted_iota(jnp.int32, (rows // 2, rows), 0) + n * rows // 2
            order = (sorted_at == position).astype(jnp.float32).astype(jnp.bfloat16)
            in_order[here, :] = jnp.dot(order, unit[...], preferred_element_type=jnp.float32).astype(jnp.bfloat16)
            while sent < AHEAD and (sent + 1) * 2 * piece <= (n + 1) * rows // 2:
                for way in range(2):
                    raw_copy(way, sent).start()
                sent += 1

    set_places(0, index, slot)
    send_all(0, unit, 0)
    flags[...] = jnp.where(lax.broadcasted_iota(jnp.int32, (8, 128), 0) == 0, pair_ref[0, 0], pair_ref[0, 1]).astype(jnp.float32)
    flag_copies = []
    for n, shift in enumerate((-1, half_way)):
        copy = pltpu.make_async_remote_copy(
            src_ref=flags, dst_ref=flags_in.at[n], send_sem=flag_ss.at[n], recv_sem=flag_rs.at[n],
            device_id=at_group(shift), device_id_type=MESH)
        copy.start()
        flag_copies.append(copy)

    def near_copy(i):
        here = pl.ds(i * chunk, chunk)
        return pltpu.make_async_remote_copy(
            src_ref=members.at[here], dst_ref=near.at[here], send_sem=near_ss.at[i], recv_sem=near_rs.at[i],
            device_id=at_group(step), device_id_type=MESH)

    @pl.when(takes_far)
    def _():
        base_copy.wait_recv()
        base = base_in[:, 0:1].astype(jnp.int32)
        position = lax.broadcasted_iota(jnp.int32, (32, rows), 1)
        begun = base <= position
        far_index = jnp.sum(jnp.where(begun, 1, 0), axis=0, keepdims=True) - 1
        far_slot = position[0:1, :] - jnp.max(jnp.where(begun, base, 0), axis=0, keepdims=True)
        set_places(1, far_index, far_slot)

    def send_near(table, k):
        for i in range(table[k - 1] if k else 0, table[k] if k < PIECES else CHIPS):
            if i:
                chunk_arrived(0, i)
            near_copy(i).start()

    for k in range(PIECES):
        @pl.when(sends_far)
        def _(k=k):
            for way in range(2):
                raw_copy(way, k).wait_recv()
                hop_copy(way, k).start()
                if k + AHEAD < PIECES:
                    raw_copy(way, k + AHEAD).start()
            send_near(NEAR_SENDER, k)

        @pl.when(takes_far)
        def _(k=k):
            for way in range(2):
                hop_copy(way, k).wait_recv()
            if k + 1 in EARLY:
                give_sibling(1, unit_in, EARLY.index(k + 1), (k + 1) * 2 * piece)
            if k in EARLY:
                make_part(1, unit_in, EARLY.index(k), k * 2 * piece)
                for h in range(2):
                    send_half(1, EARLY.index(k), h)
            send_near(NEAR_TAKER, k)

    @pl.when(sends_far)
    def _():
        send_near(NEAR_SENDER, PIECES)

    @pl.when(takes_far)
    def _():
        send_near(NEAR_TAKER, PIECES)
        send_all(1, unit_in, len(EARLY))

    tiles = 4
    height = total // tiles
    per_tile = CHIPS // tiles
    first_lane = (lax.broadcasted_iota(jnp.int32, (8, 128), 1) == 0).astype(jnp.float32).astype(jnp.bfloat16)
    marks = lax.dot_general(first_lane, members[:, 0:128], (((1,), (1,)), ((), ())), preferred_element_type=jnp.float32)
    col_bias = jnp.where(marks[0:1, :] > 2.0, DEAD, 0.0)

    def product(block, t, kept, column_best):
        self_block = kept is None
        left_at = pl.ds(t * height if isinstance(t, int) else pl.multiple_of(t * height, height), height)
        left = block[left_at, :]
        row_bias = jnp.where(block[left_at, 0:128].astype(jnp.float32)[:, 0:1] > 2.0, DEAD, 0.0)
        row_bias = jnp.broadcast_to(row_bias, (height, COLS))
        lane_best = None
        for n in range(total // COLS):
            cols = slice(n * COLS, (n + 1) * COLS)
            sim = lax.dot_general(left, members[cols, :], (((1,), (1,)), ((), ())), preferred_element_type=jnp.float32)
            down = sim + row_bias
            if self_block:
                row_id = t * height + lax.broadcasted_iota(jnp.int32, (height, COLS), 0)
                col_id = n * COLS + lax.broadcasted_iota(jnp.int32, (height, COLS), 1)
                down = jnp.where(row_id == col_id, DEAD, down)
            else:
                across = sim + col_bias[:, cols]
                across = jnp.maximum(across[:, 0:128], across[:, 128:256])
                lane_best = across if lane_best is None else jnp.maximum(lane_best, across)
            down = jnp.max(down.reshape(height // 8, 8, COLS), axis=0)
            column_best[:, cols] = jnp.maximum(column_best[:, cols], down)
        if not self_block:
            kept[left_at, :] = lane_best

    def fold(kept, into, t):
        for b in range(t * height // 128, (t + 1) * height // 128):
            lanes = slice(b * 128, (b + 1) * 128)
            into[:, lanes] = jnp.max(kept[lanes, :].T, axis=0, keepdims=True)

    best[...] = jnp.full(best.shape, DEAD, jnp.float32)

    def own_tile(t, carry):
        product(members, t, None, best.at[0])
        return carry

    lax.fori_loop(0, tiles, own_tile, 0)

    for copy in flag_copies:
        copy.wait()
    near_on = jnp.where(core == 0, flags[0:1, 0:1], flags_in[0, 0:1, 0:1])
    far_on = jnp.maximum(flags[1:2, 0:1], flags_in[1, 1:2, 0:1])

    near_back = pltpu.make_async_remote_copy(
        src_ref=back_out.at[0], dst_ref=back_in, send_sem=back_sem.at[0], recv_sem=back_sem.at[1],
        device_id=at_group(-step), device_id_type=MESH)

    def ret_copy(turn, j):
        off, to_core = OFFSETS[j // 2], (core, other)[j % 2]
        to_group = lax.rem(group + half_way, groups) if turn else group
        return pltpu.make_async_remote_copy(
            src_ref=ret_out.at[turn, j], dst_ref=ret_in.at[turn, j], send_sem=ret_ss.at[turn, j], recv_sem=ret_rs.at[turn, j],
            device_id=(to_group, chip_dev(off, -1, to_core)), device_id_type=MESH)

    ret_out[...] = jnp.zeros(ret_out.shape, jnp.float32)

    for t in range(tiles):
        for i in range(t * per_tile, (t + 1) * per_tile):
            near_copy(i).wait_recv()
        product(near, t, partial.at[0], best.at[1])
        fold(partial.at[0], back_out.at[0], t)
        if t == tiles - 1:
            back_out[0] = jnp.where(near_on > 0.5, back_out[0], -2.0)
            near_back.start()

        @pl.when(takes_far)
        def _(t=t):
            for i in range(max(1, t * per_tile), (t + 1) * per_tile):
                chunk_arrived(1, i)
            product(far, t, partial.at[1], best.at[2])
            fold(partial.at[1], back_out.at[1], t)
            for j in range(t * height // 128 * 128 // cap, (t + 1) * height // 128 * 128 // cap):
                ret_out[1, j, 0:1, 0:cap] = jnp.where(far_on > 0.5, back_out[1, :, j * cap:(j + 1) * cap], -2.0)
                ret_copy(1, j).start()

    @pl.when(takes_far)
    def _():
        ret_in[1] = jnp.full(ret_in.shape[1:], -2.0, jnp.float32)

    near_back.wait_recv()
    leading = jnp.maximum(jnp.max(best[0], axis=0, keepdims=True), -1.0)
    leading = jnp.maximum(leading, jnp.where(near_on > 0.5, jnp.max(best[1], axis=0, keepdims=True), -2.0))
    leading = jnp.maximum(leading, jnp.where(far_on > 0.5, jnp.max(best[2], axis=0, keepdims=True), -2.0))
    leading = jnp.maximum(leading, back_in[...])

    for j in range(2 * CHIPS):
        ret_out[0, j, 0:1, 0:cap] = leading[:, j * cap:(j + 1) * cap]
        if j:
            ret_copy(0, j).start()
    ret_in[0, 0] = ret_out[0, 0]

    wanted = jnp.concatenate([chosen.astype(jnp.bfloat16)] * 3, axis=0)
    pick = lax.broadcasted_iota(jnp.int32, (128, rows), 0) == slot
    for j in range(1, 2 * CHIPS):
        ret_copy(0, j).wait_recv()

    @pl.when(sends_far)
    def _():
        for j in range(2 * CHIPS):
            ret_copy(1, j).wait_recv()

    got = jnp.maximum(ret_in[0, :, 0, :], ret_in[1, :, 0, :])
    parts = []
    for _ in range(3):
        part = got.astype(jnp.bfloat16)
        got = got - part.astype(jnp.float32)
        parts.append(part)
    spread = lax.dot_general(
        jnp.concatenate(parts, axis=0), wanted, (((0,), (0,)), ((), ())), preferred_element_type=jnp.float32)
    out_ref[...] = jnp.sum(jnp.where(pick, spread, 0.0), axis=0)

    near_back.wait_send()
    for j in range(1, 2 * CHIPS):
        ret_copy(0, j).wait_send()
    for i in range(CHIPS):
        near_copy(i).wait_send()
        if i:
            chunk_left(0, i)

    @pl.when(sends_far)
    def _():
        for k in range(PIECES):
            for way in range(2):
                raw_copy(way, k).wait_send()
                hop_copy(way, k).wait_send()
        base_copy.wait_send()

    @pl.when(takes_far)
    def _():
        for i in range(1, CHIPS):
            chunk_left(1, i)
        for j in range(2 * CHIPS):
            ret_copy(1, j).wait_send()


def on_device(embeddings, assignment, owner_of, pair_on):
    rows, width = embeddings.shape
    owners = owner_of.shape[0]
    cap = 2 * rows // owners
    total = owners * cap
    half = total // 2
    bf16, f32 = jnp.bfloat16, jnp.float32
    dma = pltpu.SemaphoreType.DMA
    out = pl.pallas_call(
        functools.partial(kernel, cap),
        out_shape=jax.ShapeDtypeStruct((rows,), f32),
        in_specs=[pl.BlockSpec(memory_space=pltpu.VMEM)] * 2 + [pl.BlockSpec(memory_space=pltpu.SMEM)] * 2,
        out_specs=pl.BlockSpec(memory_space=pltpu.VMEM),
        scratch_shapes=[
            pltpu.VMEM((rows, width), bf16),
            pltpu.VMEM((rows, width), bf16),
            pltpu.VMEM((2, 2, 1, rows), jnp.int32),
            pltpu.VMEM((2, half, width), bf16),
            pltpu.VMEM((2, half, width), bf16),
            pltpu.VMEM((2, total, width), bf16),
            pltpu.VMEM((total, width), bf16),
            pltpu.VMEM((total, width), bf16),
            pltpu.VMEM((total, width), bf16),
            pltpu.VMEM((owners, 128), f32),
            pltpu.VMEM((2, PIECES, rows // (2 * PIECES), width), bf16),
            pltpu.VMEM((rows, width), bf16),
            pltpu.VMEM((owners, 128), f32),
            pltpu.VMEM((3, 8, total), f32),
            pltpu.VMEM((2, total, 128), f32),
            pltpu.VMEM((2, 1, total), f32),
            pltpu.VMEM((1, total), f32),
            pltpu.VMEM((8, 128), f32),
            pltpu.VMEM((2, 8, 128), f32),
            pltpu.VMEM((2, owners, 1, 128), f32),
            pltpu.VMEM((2, owners, 1, 128), f32),
            dma((2, 6)), dma((2, 6)),
            dma((2, CHIPS, 2)), dma((2, CHIPS, 2)),
            dma((CHIPS,)), dma((CHIPS,)),
            dma((2, PIECES)), dma((2, PIECES)),
            dma((2, PIECES)), dma((2, PIECES)),
            dma((2,)),
            dma((2,)),
            dma((2,)), dma((2,)),
            dma((2, owners)), dma((2, owners)),
        ],
        compiler_params=pltpu.CompilerParams(
            collective_id=0, has_side_effects=True, vmem_limit_bytes=56 * 2**20),
        cost_estimate=pl.CostEstimate(flops=6 * total * total * width, bytes_accessed=2 * rows * width, transcendentals=0),
        name="semdedup",
    )(embeddings, assignment.reshape(1, rows), owner_of, pair_on.reshape(1, 2))
    return out


def solution(mesh):
    placed = (P(("group", "dev"), None), P(("group", "dev"), None), P(), P(None, ("group", "dev")))
    return jax.shard_map(
        on_device, mesh=mesh, in_specs=placed, out_specs=P(("group", "dev")), check_vma=False
    )
```

```python
import functools

import jax
import jax.numpy as jnp
from jax import lax
from jax.experimental import pallas as pl
from jax.experimental.pallas import tpu as pltpu
from jax.sharding import PartitionSpec as P

MESH = pl.DeviceIdType.MESH
SIDE = 4
CHIPS = SIDE * SIDE
OFFSETS = (
    (0, 0), (2, 2), (1, 2), (2, 1), (3, 2), (2, 3), (1, 1), (3, 3),
    (1, 3), (3, 1), (2, 0), (0, 2), (1, 0), (0, 1), (3, 0), (0, 3),
)
MARK = 4.0
DEAD = -8.0
COLS = 256
PIECES = 7
AHEAD = 7
NEAR_SENDER = (0, 0, 0, 0, 0, 0, 0)
NEAR_TAKER = (0, 0, 0, 0, 6, 11, 16)
PARTS = (((0, 4), (4, 8), (8, 12), (12, 16)), ((0, 2), (2, 4), (4, 6), (6, 8), (8, 12), (12, 16)))
EARLY = (2, 4, 6)


def kernel(cap, emb_ref, assign_ref, owner_of_ref, pair_ref, out_ref,
           unit, in_order, place, sib_out, sib_in, outbox, members, near, far,
           base_out, relayed, unit_in, base_in,
           best, partial, back_out, back_in, flags, flags_in, ret_out, ret_in,
           sib_ss, sib_rs, a2a_ss, a2a_rs, near_ss, near_rs, raw_ss, raw_rs, hop_ss, hop_rs, base_sem,
           back_sem, flag_ss, flag_rs, ret_ss, ret_rs):
    rows, width = emb_ref.shape
    chunk = 2 * cap
    total = CHIPS * chunk
    group = lax.axis_index("group")
    dev = lax.axis_index("dev")
    groups = lax.axis_size("group")
    core = lax.rem(dev, 2)
    y = lax.rem(dev // 2, SIDE)
    x = dev // (2 * SIDE)

    def chip_dev(off, sign, to_core):
        cx = lax.rem(x + sign * off[0] + SIDE, SIDE)
        cy = lax.rem(y + sign * off[1] + SIDE, SIDE)
        return (cx * SIDE + cy) * 2 + to_core

    def at_group(shift):
        return (lax.rem(group + shift + groups, groups), dev)

    other = 1 - core
    step = 1 - 2 * core
    half_way = groups // 2

    def any_of(*numbers):
        hit = group == numbers[0]
        for number in numbers[1:]:
            hit = hit | (group == number)
        return hit

    def by_group(table):
        return sum((group == g).astype(jnp.int32) * value for g, value in table.items())

    ways = ({0: 2, 2: 5, 5: 7, 7: 0}, {0: 7, 7: 5, 5: 2, 2: 0})
    sends_far = any_of(0, 2, 5, 7)
    takes_far = any_of(1, 3, 4, 6)
    first_hop = [by_group(way) for way in ways]
    second_hop = [by_group({way[g]: (g + half_way) % groups for g in way}) for way in ways]
    came_from = [by_group({(g + half_way) % groups: way[g] for g in way}) for way in ways]

    barrier = pltpu.get_barrier_semaphore()
    for i, off in enumerate(OFFSETS):
        if i:
            pl.semaphore_signal(barrier, inc=1, device_id=(group, chip_dev(off, 1, core)), device_id_type=MESH)
        pl.semaphore_signal(barrier, inc=1, device_id=(group, chip_dev(off, 1, other)), device_id_type=MESH)
    pl.semaphore_signal(barrier, inc=1, device_id=at_group(half_way), device_id_type=MESH)
    for shift in (1, -1):
        pl.semaphore_signal(barrier, inc=1, device_id=at_group(shift), device_id_type=MESH)

    @pl.when(sends_far)
    def _():
        for way in range(2):
            pl.semaphore_signal(barrier, inc=1, device_id=(first_hop[way], dev), device_id_type=MESH)
            pl.semaphore_signal(barrier, inc=2, device_id=(second_hop[way], dev), device_id_type=MESH)
        far_group = lax.rem(group + half_way, groups)
        for i, off in enumerate(OFFSETS):
            for to_core in (core, other):
                if i or to_core is other:
                    pl.semaphore_signal(barrier, inc=1, device_id=(far_group, chip_dev(off, 1, to_core)), device_id_type=MESH)

    @pl.when(takes_far)
    def _():
        for way in range(2):
            pl.semaphore_signal(barrier, inc=1, device_id=(came_from[way], dev), device_id_type=MESH)

    values = emb_ref[...].astype(jnp.float32)
    unit[...] = (values * lax.rsqrt(jnp.sum(values * values, axis=1, keepdims=True) + 1e-06)).astype(jnp.bfloat16)

    assign = assign_ref[...]
    ids = lax.broadcasted_iota(jnp.int32, (32, rows), 0)
    owner = jnp.zeros((1, rows), jnp.int32)
    for n in range(owner_of_ref.shape[0]):
        owner = jnp.where(assign == n, owner_of_ref[n], owner)
    index = jnp.full((1, rows), -1, jnp.int32)
    for i, off in enumerate(OFFSETS):
        for q, to_core in enumerate((core, other)):
            index = jnp.where(owner == chip_dev(off, 1, to_core), 2 * i + q, index)
    chosen = (index == ids).astype(jnp.float32)
    before = (lax.broadcasted_iota(jnp.int32, (128, 128), 0)
              < lax.broadcasted_iota(jnp.int32, (128, 128), 1)).astype(jnp.float32).astype(jnp.bfloat16)
    blocks = [chosen[:, n * 128:(n + 1) * 128] for n in range(rows // 128)]
    counted = jnp.dot(jnp.concatenate(blocks, axis=0).astype(jnp.bfloat16), before, preferred_element_type=jnp.float32)
    earlier = jnp.zeros((32, 1), jnp.float32)
    slots = []
    for n, block in enumerate(blocks):
        inside = counted[n * 32:(n + 1) * 32, :] + earlier
        slots.append(jnp.sum(inside * block, axis=0, keepdims=True))
        earlier = earlier + jnp.sum(block, axis=1, keepdims=True)
    slot = jnp.concatenate(slots, axis=1).astype(jnp.int32)
    above = (lax.broadcasted_iota(jnp.int32, (32, 32), 1)
             < lax.broadcasted_iota(jnp.int32, (32, 32), 0)).astype(jnp.float32).astype(jnp.bfloat16)
    base_out[...] = jnp.dot(
        above, jnp.broadcast_to(earlier, (32, 128)).astype(jnp.bfloat16), preferred_element_type=jnp.float32)

    piece = rows // (2 * PIECES)

    def raw_copy(way, k):
        return pltpu.make_async_remote_copy(
            src_ref=in_order.at[pl.ds((2 * k + way) * piece, piece)], dst_ref=relayed.at[way, k],
            send_sem=raw_ss.at[way, k], recv_sem=raw_rs.at[way, k],
            device_id=(first_hop[way], dev), device_id_type=MESH)

    def hop_copy(way, k):
        return pltpu.make_async_remote_copy(
            src_ref=relayed.at[way, k], dst_ref=unit_in.at[pl.ds((2 * k + way) * piece, piece)],
            send_sem=hop_ss.at[way, k], recv_sem=hop_rs.at[way, k],
            device_id=(second_hop[way], dev), device_id_type=MESH)

    base_copy = pltpu.make_async_remote_copy(
        src_ref=base_out, dst_ref=base_in, send_sem=base_sem.at[0], recv_sem=base_sem.at[1],
        device_id=at_group(half_way), device_id_type=MESH)

    def set_places(turn, index, slot):
        for q in range(2):
            place[turn, q] = jnp.where(index % 2 == q, index // 2 * cap + slot, -1)

    def packed(turn, q, source, part, depth):
        position = lax.broadcasted_iota(jnp.int32, ((part[1] - part[0]) * cap, depth), 0) + part[0] * cap
        hits = (place[turn, q, :, 0:depth] == position).astype(jnp.float32)
        live = jnp.sum(hits, axis=1, keepdims=True)
        got = jnp.dot(hits.astype(jnp.bfloat16), source[0:depth, :], preferred_element_type=jnp.float32)
        lane = lax.broadcasted_iota(jnp.int32, got.shape, 1)
        return jnp.where((lane == 0) & (live < 0.5), MARK, got)

    def sib_copy(turn, n):
        first, last = PARTS[turn][n]
        here = pl.ds(first * cap, (last - first) * cap)
        return pltpu.make_async_remote_copy(
            src_ref=sib_out.at[turn, here], dst_ref=sib_in.at[turn, here],
            send_sem=sib_ss.at[turn, n], recv_sem=sib_rs.at[turn, n],
            device_id=(group, chip_dev((0, 0), 1, other)), device_id_type=MESH)

    cut = -(-chunk // 32) * 16

    def chunk_copy(turn, i, h):
        here = pl.ds(i * chunk + h * cut, chunk - cut if h else cut)
        return pltpu.make_async_remote_copy(
            src_ref=outbox.at[turn, here], dst_ref=(members, far)[turn].at[here],
            send_sem=a2a_ss.at[turn, i, h], recv_sem=a2a_rs.at[turn, i, h],
            device_id=(group, chip_dev(OFFSETS[i], 1, core)), device_id_type=MESH)

    def chunk_arrived(turn, i):
        for h in range(2):
            chunk_copy(turn, i, h).wait_recv()

    def chunk_left(turn, i):
        for h in range(2):
            chunk_copy(turn, i, h).wait_send()

    def give_sibling(turn, source, n, depth=rows):
        part = PARTS[turn][n]
        sib_out[turn, part[0] * cap:part[1] * cap, :] = packed(turn, 1, source, part, depth).astype(jnp.bfloat16)
        sib_copy(turn, n).start()

    def make_part(turn, source, n, depth=rows):
        part = PARTS[turn][n]
        own = packed(turn, 0, source, part, depth)
        sib_copy(turn, n).wait()
        from_sib = sib_in[turn, part[0] * cap:part[1] * cap, :].astype(jnp.float32)
        for i in range(*part):
            here = slice((i - part[0]) * cap, (i - part[0] + 1) * cap)
            both = jnp.concatenate([own[here, :], from_sib[here, :]], axis=0).astype(jnp.bfloat16)
            if i == 0:
                (members, far)[turn][0:chunk, :] = both
            else:
                outbox[turn, i * chunk:(i + 1) * chunk, :] = both

    def send_half(turn, n, h):
        for i in range(*PARTS[turn][n]):
            if i:
                chunk_copy(turn, i, h).start()

    def send_all(turn, source, first):
        last = len(PARTS[turn])
        for n in range(first, min(first + 2, last)):
            give_sibling(turn, source, n)
        for n in range(first, last):
            make_part(turn, source, n)
            send_half(turn, n, 0)
            if n + 2 < last:
                give_sibling(turn, source, n + 2)
        for n in range(first, last):
            send_half(turn, n, 1)

    pl.semaphore_wait(barrier, 2 * CHIPS - 1 + 1 + 2 + 4 + (2 * CHIPS - 1) * takes_far.astype(jnp.int32))

    @pl.when(sends_far)
    def _():
        base_copy.start()
        sorted_at = jnp.sum(chosen * base_out[:, 0:1], axis=0, keepdims=True).astype(jnp.int32) + slot
        sent = 0
        for n in range(2):
            here = slice(n * rows // 2, (n + 1) * rows // 2)
            position = lax.broadcasted_iota(jnp.int32, (rows // 2, rows), 0) + n * rows // 2
            order = (sorted_at == position).astype(jnp.float32).astype(jnp.bfloat16)
            in_order[here, :] = jnp.dot(order, unit[...], preferred_element_type=jnp.float32).astype(jnp.bfloat16)
            while sent < AHEAD and (sent + 1) * 2 * piece <= (n + 1) * rows // 2:
                for way in range(2):
                    raw_copy(way, sent).start()
                sent += 1

    set_places(0, index, slot)
    send_all(0, unit, 0)
    flags[...] = jnp.where(lax.broadcasted_iota(jnp.int32, (8, 128), 0) == 0, pair_ref[0, 0], pair_ref[0, 1]).astype(jnp.float32)
    flag_copies = []
    for n, shift in enumerate((-1, half_way)):
        copy = pltpu.make_async_remote_copy(
            src_ref=flags, dst_ref=flags_in.at[n], send_sem=flag_ss.at[n], recv_sem=flag_rs.at[n],
            device_id=at_group(shift), device_id_type=MESH)
        copy.start()
        flag_copies.append(copy)

    def near_copy(i):
        here = pl.ds(i * chunk, chunk)
        return pltpu.make_async_remote_copy(
            src_ref=members.at[here], dst_ref=near.at[here], send_sem=near_ss.at[i], recv_sem=near_rs.at[i],
            device_id=at_group(step), device_id_type=MESH)

    @pl.when(takes_far)
    def _():
        base_copy.wait_recv()
        base = base_in[:, 0:1].astype(jnp.int32)
        position = lax.broadcasted_iota(jnp.int32, (32, rows), 1)
        begun = base <= position
        far_index = jnp.sum(jnp.where(begun, 1, 0), axis=0, keepdims=True) - 1
        far_slot = position[0:1, :] - jnp.max(jnp.where(begun, base, 0), axis=0, keepdims=True)
        set_places(1, far_index, far_slot)

    def send_near(table, k):
        for i in range(table[k - 1] if k else 0, table[k] if k < PIECES else CHIPS):
            if i:
                chunk_arrived(0, i)
            near_copy(i).start()

    for k in range(PIECES):
        @pl.when(sends_far)
        def _(k=k):
            for way in range(2):
                raw_copy(way, k).wait_recv()
                hop_copy(way, k).start()
                if k + AHEAD < PIECES:
                    raw_copy(way, k + AHEAD).start()
            send_near(NEAR_SENDER, k)

        @pl.when(takes_far)
        def _(k=k):
            for way in range(2):
                hop_copy(way, k).wait_recv()
            if k + 1 in EARLY:
                give_sibling(1, unit_in, EARLY.index(k + 1), (k + 1) * 2 * piece)
                make_part(1, unit_in, EARLY.index(k + 1), (k + 1) * 2 * piece)
                for h in range(2):
                    send_half(1, EARLY.index(k + 1), h)
            send_near(NEAR_TAKER, k)

    @pl.when(sends_far)
    def _():
        send_near(NEAR_SENDER, PIECES)

    @pl.when(takes_far)
    def _():
        send_near(NEAR_TAKER, PIECES)
        send_all(1, unit_in, len(EARLY))

    tiles = 4
    height = total // tiles
    per_tile = CHIPS // tiles
    first_lane = (lax.broadcasted_iota(jnp.int32, (8, 128), 1) == 0).astype(jnp.float32).astype(jnp.bfloat16)
    marks = lax.dot_general(first_lane, members[:, 0:128], (((1,), (1,)), ((), ())), preferred_element_type=jnp.float32)
    col_bias = jnp.where(marks[0:1, :] > 2.0, DEAD, 0.0)

    def product(block, t, kept, column_best):
        self_block = kept is None
        left_at = pl.ds(t * height if isinstance(t, int) else pl.multiple_of(t * height, height), height)
        left = block[left_at, :]
        row_bias = jnp.where(block[left_at, 0:128].astype(jnp.float32)[:, 0:1] > 2.0, DEAD, 0.0)
        row_bias = jnp.broadcast_to(row_bias, (height, COLS))
        lane_best = None
        for n in range(total // COLS):
            cols = slice(n * COLS, (n + 1) * COLS)
            sim = lax.dot_general(left, members[cols, :], (((1,), (1,)), ((), ())), preferred_element_type=jnp.float32)
            down = sim + row_bias
            if self_block:
                row_id = t * height + lax.broadcasted_iota(jnp.int32, (height, COLS), 0)
                col_id = n * COLS + lax.broadcasted_iota(jnp.int32, (height, COLS), 1)
                down = jnp.where(row_id == col_id, DEAD, down)
            else:
                across = sim + col_bias[:, cols]
                across = jnp.maximum(across[:, 0:128], across[:, 128:256])
                lane_best = across if lane_best is None else jnp.maximum(lane_best, across)
            down = jnp.max(down.reshape(height // 8, 8, COLS), axis=0)
            column_best[:, cols] = jnp.maximum(column_best[:, cols], down)
        if not self_block:
            kept[left_at, :] = lane_best

    def fold(kept, into, t):
        for b in range(t * height // 128, (t + 1) * height // 128):
            lanes = slice(b * 128, (b + 1) * 128)
            into[:, lanes] = jnp.max(kept[lanes, :].T, axis=0, keepdims=True)

    best[...] = jnp.full(best.shape, DEAD, jnp.float32)

    def own_tile(t, carry):
        product(members, t, None, best.at[0])
        return carry

    lax.fori_loop(0, tiles, own_tile, 0)

    for copy in flag_copies:
        copy.wait()
    near_on = jnp.where(core == 0, flags[0:1, 0:1], flags_in[0, 0:1, 0:1])
    far_on = jnp.maximum(flags[1:2, 0:1], flags_in[1, 1:2, 0:1])

    near_back = pltpu.make_async_remote_copy(
        src_ref=back_out.at[0], dst_ref=back_in, send_sem=back_sem.at[0], recv_sem=back_sem.at[1],
        device_id=at_group(-step), device_id_type=MESH)

    def ret_copy(turn, j):
        off, to_core = OFFSETS[j // 2], (core, other)[j % 2]
        to_group = lax.rem(group + half_way, groups) if turn else group
        return pltpu.make_async_remote_copy(
            src_ref=ret_out.at[turn, j], dst_ref=ret_in.at[turn, j], send_sem=ret_ss.at[turn, j], recv_sem=ret_rs.at[turn, j],
            device_id=(to_group, chip_dev(off, -1, to_core)), device_id_type=MESH)

    ret_out[...] = jnp.zeros(ret_out.shape, jnp.float32)

    for t in range(tiles):
        for i in range(t * per_tile, (t + 1) * per_tile):
            near_copy(i).wait_recv()
        product(near, t, partial.at[0], best.at[1])
        fold(partial.at[0], back_out.at[0], t)
        if t == tiles - 1:
            back_out[0] = jnp.where(near_on > 0.5, back_out[0], -2.0)
            near_back.start()

        @pl.when(takes_far)
        def _(t=t):
            for i in range(max(1, t * per_tile), (t + 1) * per_tile):
                chunk_arrived(1, i)
            product(far, t, partial.at[1], best.at[2])
            fold(partial.at[1], back_out.at[1], t)
            for j in range(t * height // 128 * 128 // cap, (t + 1) * height // 128 * 128 // cap):
                ret_out[1, j, 0:1, 0:cap] = jnp.where(far_on > 0.5, back_out[1, :, j * cap:(j + 1) * cap], -2.0)
                ret_copy(1, j).start()

    @pl.when(takes_far)
    def _():
        ret_in[1] = jnp.full(ret_in.shape[1:], -2.0, jnp.float32)

    near_back.wait_recv()
    leading = jnp.maximum(jnp.max(best[0], axis=0, keepdims=True), -1.0)
    leading = jnp.maximum(leading, jnp.where(near_on > 0.5, jnp.max(best[1], axis=0, keepdims=True), -2.0))
    leading = jnp.maximum(leading, jnp.where(far_on > 0.5, jnp.max(best[2], axis=0, keepdims=True), -2.0))
    leading = jnp.maximum(leading, back_in[...])

    for j in range(2 * CHIPS):
        ret_out[0, j, 0:1, 0:cap] = leading[:, j * cap:(j + 1) * cap]
        if j:
            ret_copy(0, j).start()
    ret_in[0, 0] = ret_out[0, 0]

    wanted = jnp.concatenate([chosen.astype(jnp.bfloat16)] * 3, axis=0)
    pick = lax.broadcasted_iota(jnp.int32, (128, rows), 0) == slot
    for j in range(1, 2 * CHIPS):
        ret_copy(0, j).wait_recv()

    @pl.when(sends_far)
    def _():
        for j in range(2 * CHIPS):
            ret_copy(1, j).wait_recv()

    got = jnp.maximum(ret_in[0, :, 0, :], ret_in[1, :, 0, :])
    parts = []
    for _ in range(3):
        part = got.astype(jnp.bfloat16)
        got = got - part.astype(jnp.float32)
        parts.append(part)
    spread = lax.dot_general(
        jnp.concatenate(parts, axis=0), wanted, (((0,), (0,)), ((), ())), preferred_element_type=jnp.float32)
    out_ref[...] = jnp.sum(jnp.where(pick, spread, 0.0), axis=0)

    near_back.wait_send()
    for j in range(1, 2 * CHIPS):
        ret_copy(0, j).wait_send()
    for i in range(CHIPS):
        near_copy(i).wait_send()
        if i:
            chunk_left(0, i)

    @pl.when(sends_far)
    def _():
        for k in range(PIECES):
            for way in range(2):
                raw_copy(way, k).wait_send()
                hop_copy(way, k).wait_send()
        base_copy.wait_send()

    @pl.when(takes_far)
    def _():
        for i in range(1, CHIPS):
            chunk_left(1, i)
        for j in range(2 * CHIPS):
            ret_copy(1, j).wait_send()


def on_device(embeddings, assignment, owner_of, pair_on):
    rows, width = embeddings.shape
    owners = owner_of.shape[0]
    cap = 2 * rows // owners
    total = owners * cap
    half = total // 2
    bf16, f32 = jnp.bfloat16, jnp.float32
    dma = pltpu.SemaphoreType.DMA
    out = pl.pallas_call(
        functools.partial(kernel, cap),
        out_shape=jax.ShapeDtypeStruct((rows,), f32),
        in_specs=[pl.BlockSpec(memory_space=pltpu.VMEM)] * 2 + [pl.BlockSpec(memory_space=pltpu.SMEM)] * 2,
        out_specs=pl.BlockSpec(memory_space=pltpu.VMEM),
        scratch_shapes=[
            pltpu.VMEM((rows, width), bf16),
            pltpu.VMEM((rows, width), bf16),
            pltpu.VMEM((2, 2, 1, rows), jnp.int32),
            pltpu.VMEM((2, half, width), bf16),
            pltpu.VMEM((2, half, width), bf16),
            pltpu.VMEM((2, total, width), bf16),
            pltpu.VMEM((total, width), bf16),
            pltpu.VMEM((total, width), bf16),
            pltpu.VMEM((total, width), bf16),
            pltpu.VMEM((owners, 128), f32),
            pltpu.VMEM((2, PIECES, rows // (2 * PIECES), width), bf16),
            pltpu.VMEM((rows, width), bf16),
            pltpu.VMEM((owners, 128), f32),
            pltpu.VMEM((3, 8, total), f32),
            pltpu.VMEM((2, total, 128), f32),
            pltpu.VMEM((2, 1, total), f32),
            pltpu.VMEM((1, total), f32),
            pltpu.VMEM((8, 128), f32),
            pltpu.VMEM((2, 8, 128), f32),
            pltpu.VMEM((2, owners, 1, 128), f32),
            pltpu.VMEM((2, owners, 1, 128), f32),
            dma((2, 6)), dma((2, 6)),
            dma((2, CHIPS, 2)), dma((2, CHIPS, 2)),
            dma((CHIPS,)), dma((CHIPS,)),
            dma((2, PIECES)), dma((2, PIECES)),
            dma((2, PIECES)), dma((2, PIECES)),
            dma((2,)),
            dma((2,)),
            dma((2,)), dma((2,)),
            dma((2, owners)), dma((2, owners)),
        ],
        compiler_params=pltpu.CompilerParams(
            collective_id=0, has_side_effects=True, vmem_limit_bytes=56 * 2**20),
        cost_estimate=pl.CostEstimate(flops=6 * total * total * width, bytes_accessed=2 * rows * width, transcendentals=0),
        name="semdedup",
    )(embeddings, assignment.reshape(1, rows), owner_of, pair_on.reshape(1, 2))
    return out


def solution(mesh):
    placed = (P(("group", "dev"), None), P(("group", "dev"), None), P(), P(None, ("group", "dev")))
    return jax.shard_map(
        on_device, mesh=mesh, in_specs=placed, out_specs=P(("group", "dev")), check_vma=False
    )
```
